1024 devices in a mesh: shard: 128 (over z, y), replica: 8 (over x, core).
Axes of the slice: x: 4, y: 4, z: 32, core: 2. Of those that a mesh axis runs over, the one named last changes fastest.
Arguments:
- replica_grads: bfloat16 [8, 4096, 6144], P('replica', 'shard'), may hold values from -5 to 5
- block_row: int32 [96], replicated, may hold values from 0 to 7, as said below
- block_col: int32 [96], replicated, may hold values from 0 to 11, as said below
- block_owner: int32 [96], replicated, may hold values from 0 to 127, as said below
- left_stats: float32 [256, 512, 512], P('shard', 'replica'), as said below
- right_stats: float32 [256, 512, 512], P('shard', 'replica'), as said below
- left_root: bfloat16 [256, 512, 512], P('shard'), as said below
- right_root: bfloat16 [256, 512, 512], P('shard'), as said below
Outputs:
- direction: bfloat16 [256, 512, 512], P('shard', 'replica')
- left_next: float32 [256, 512, 512], P('shard', 'replica')
- right_next: float32 [256, 512, 512], P('shard', 'replica')
The draws below stay inside these ranges and needn't reach their ends.
Inputs may be any that keep to these rules, and one draw needn't show every extreme that they name: block_row and block_col together name each of the 8 x 12 block positions exactly once. `block_col`: see block_row. `block_owner`: no shard index owns more than 2 blocks, and some index owns exactly 2. `left_stats`: symmetric. `right_stats`: symmetric. `left_root`: symmetric. `right_root`: symmetric.
All inputs are finite; a program needn't handle non-finite values.
Results may differ from the reference program's by a relative error of at most 0.022.
Values may be sent and summed in bfloat16 or wider, within the bound.
No kernel may reach another device: no remote copies, remote signals or barrier semaphores. Data moves between devices by JAX's collectives and lax.ppermute only.
A program may use at most 64 MiB of HBM per device.

```python
import jax
import jax.numpy as jnp
from jax import lax

ROWS = 4096
COLS = 6144
BLOCK = 512
NCB = 12
BLOCKS = 96
SLOTS = 2
N_SHARD = 128
N_REPLICA = 8


def owner_layout(key):
    positions = jax.random.permutation(jax.random.fold_in(key, 11), BLOCKS).astype(jnp.int32)
    leader = jax.random.randint(jax.random.fold_in(key, 12), (), 0, N_SHARD).astype(jnp.int32)
    spots = jax.random.permutation(jax.random.fold_in(key, 13), (N_SHARD - 1) * SLOTS).astype(jnp.int32)
    order = jnp.arange(BLOCKS, dtype=jnp.int32)
    later = spots[jnp.clip(order - SLOTS, 0, (N_SHARD - 1) * SLOTS - 1)]
    holder = jnp.where(order < SLOTS, leader, (leader + 1 + later // SLOTS) % N_SHARD)
    return (positions, holder.astype(jnp.int32))


def symmetric_root(key):
    noise = jax.random.normal(jax.random.fold_in(key, 21), (N_SHARD * SLOTS, BLOCK, BLOCK), jnp.float32)
    noise = 0.02 * (noise + jnp.swapaxes(noise, 1, 2)) * 0.7071
    diagonal = jax.random.uniform(jax.random.fold_in(key, 22), (N_SHARD * SLOTS, BLOCK), jnp.float32, 0.4, 1.2)
    return noise + jnp.eye(BLOCK, dtype=jnp.float32)[None] * diagonal[:, :, None]


def stats_matrix(key, noise, diagonal):
    noise = 0.006 * (noise + jnp.swapaxes(noise, 1, 2)) * 0.7071
    return noise + jnp.eye(BLOCK, dtype=jnp.float32)[None] * diagonal[:, :, None]


def draw_block_row(key, part):
    positions, holder = owner_layout(key)
    return (positions // NCB).astype(jnp.int32)


def draw_block_col(key, part):
    positions, holder = owner_layout(key)
    return (positions % NCB).astype(jnp.int32)


def draw_block_owner(key, part):
    positions, holder = owner_layout(key)
    return holder


def draw_left_stats(key, part):
    key = jax.random.fold_in(key, 4)
    shape = (N_SHARD * SLOTS, BLOCK, BLOCK)
    noise = jax.random.normal(jax.random.fold_in(key, 31), shape, jnp.float32)
    diagonal = jax.random.uniform(jax.random.fold_in(key, 32), shape[:2], jnp.float32, 0.1, 0.4)
    return stats_matrix(key, noise, diagonal)


def draw_right_stats(key, part):
    key = jax.random.fold_in(key, 5)
    shape = (N_SHARD * SLOTS, BLOCK, BLOCK)
    noise = jax.random.normal(jax.random.fold_in(key, 31), shape, jnp.float32)
    diagonal = jax.random.uniform(jax.random.fold_in(key, 32), shape[:2], jnp.float32, 0.1, 0.4)
    return stats_matrix(key, noise, diagonal)


def draw_left_root(key, part):
    key = jax.random.fold_in(key, 2)
    return symmetric_root(key).astype(jnp.bfloat16)


def draw_right_root(key, part):
    key = jax.random.fold_in(key, 3)
    return symmetric_root(key).astype(jnp.bfloat16)


def levels(own_key, shape, pieces, smallest, high):
    def one(position, blocks):
        heights = jax.random.uniform(jax.random.fold_in(jax.random.fold_in(own_key, 6), position), (blocks,), jnp.float32, smallest / len(pieces), high / len(pieces))
        return jnp.repeat(jnp.exp(heights), shape[position] // blocks).reshape((-1,) + (1,) * (len(shape) - position - 1))

    level = one(*pieces[0])
    for cut in pieces[1:]:
        level = level * one(*cut)
    return level


def centred(stream_key, dims, deviation, most, pieces=(), kind=jnp.bfloat16):
    factor_of = levels(stream_key, dims, pieces, -0.22, 0.18) if pieces else 1.0
    entries = jax.random.normal(stream_key, dims, jnp.float32) * deviation * factor_of
    return jnp.minimum(jnp.maximum(entries, -most), most).astype(kind)


def setup_inputs(seed: int = 0) -> dict:
    keys = jax.random.split(jax.random.key(seed), 9)
    replica_grads = centred(keys[0], (N_REPLICA, ROWS, COLS), 0.35, 5.0, ((0, 8), (1, 128)))
    block_row = draw_block_row(jax.random.fold_in(keys[8], 71), 0)
    block_col = draw_block_col(jax.random.fold_in(keys[8], 71), 0)
    block_owner = draw_block_owner(jax.random.fold_in(keys[8], 71), 0)
    left_stats = draw_left_stats(jax.random.fold_in(keys[8], 71), 0)
    right_stats = draw_right_stats(jax.random.fold_in(keys[8], 71), 0)
    left_root = draw_left_root(jax.random.fold_in(keys[8], 71), 0)
    right_root = draw_right_root(jax.random.fold_in(keys[8], 71), 0)
    return dict(replica_grads=replica_grads, block_row=block_row, block_col=block_col, block_owner=block_owner, left_stats=left_stats, right_stats=right_stats, left_root=left_root, right_root=right_root)


def locate_slot(block_owner, block_row, block_col, slot_index):
    holder = slot_index // SLOTS
    within = slot_index % SLOTS
    owned = (block_owner == holder).astype(jnp.int32)
    ranking = jnp.cumsum(owned) - 1
    chosen = owned * (ranking == within).astype(jnp.int32)
    return jnp.sum(chosen), jnp.sum(chosen * block_row), jnp.sum(chosen * block_col)


def reference(replica_grads, block_row, block_col, block_owner, left_stats, right_stats, left_root, right_root):
    gradient = jnp.sum(replica_grads.astype(jnp.float32), axis=0).astype(jnp.bfloat16)

    def one_slot(slot_index):
        filled, row_index, col_index = locate_slot(block_owner, block_row, block_col, slot_index)
        chosen_block = lax.dynamic_slice(gradient, ((row_index * BLOCK).astype(jnp.int32), (col_index * BLOCK).astype(jnp.int32)), (BLOCK, BLOCK))
        chosen_block = jnp.where(filled > 0, chosen_block, jnp.zeros_like(chosen_block))
        gram_left = jnp.dot(chosen_block, chosen_block.T, preferred_element_type=jnp.float32)
        gram_right = jnp.dot(chosen_block.T, chosen_block, preferred_element_type=jnp.float32)
        left_new = 0.8 * left_stats[slot_index] + (0.2 / BLOCK) * gram_left
        right_new = 0.8 * right_stats[slot_index] + (0.2 / BLOCK) * gram_right
        mixed = jnp.dot(chosen_block, right_root[slot_index], preferred_element_type=jnp.float32).astype(jnp.bfloat16)
        direction = jnp.dot(left_root[slot_index], mixed, preferred_element_type=jnp.float32).astype(jnp.bfloat16)
        return direction, left_new, right_new

    direction, left_next, right_next = lax.map(one_slot, jnp.arange(N_SHARD * SLOTS, dtype=jnp.int32))
    return (direction, left_next, right_next)
```

```python
import jax
import jax.numpy as jnp
from jax import lax
from jax.experimental import pallas as pl
from jax.experimental.pallas import tpu as pltpu
from jax.sharding import Mesh, PartitionSpec as P

NEAR = ("zl", "y")
TILE_ROWS = 16
LANES = 128


def vmem(n):
    return [pl.BlockSpec(memory_space=pltpu.VMEM)] * n


def cut_kernel(owner_ref, row_ref, col_ref, grads_ref, parts_ref, slot_ref, count_ref, *, near, slots, ncb):
    order = grads_ref.shape[2] // ncb
    groups = order // LANES
    halves = grads_ref.shape[1] // TILE_ROWS
    for group in range(groups):
        for half in range(halves):
            for b in range(ncb):
                parts_ref[group * halves + half, b] = grads_ref[
                    0, pl.ds(half * TILE_ROWS, TILE_ROWS), pl.ds(b * order + group * LANES, LANES)
                ]
    blocks = owner_ref.shape[0]
    base = lax.axis_index("cube") * near

    def clear(i, carry):
        slot_ref[i] = -1
        return carry

    lax.fori_loop(0, slot_ref.shape[0], clear, 0)

    def reset(i, carry):
        count_ref[i] = 0
        return carry

    lax.fori_loop(0, count_ref.shape[0], reset, 0)

    def put(b, carry):
        local = owner_ref[b] - base
        mine = (local >= 0) & (local < near)

        @pl.when(mine)
        def _():
            rank = count_ref[local]
            slot_ref[local * slots + rank] = row_ref[b] * ncb + col_ref[b]
            count_ref[local] = rank + 1

        return carry

    lax.fori_loop(0, blocks, put, 0)


def pick_kernel(slot_ref, shares_ref, picked_ref):
    for s in range(picked_ref.shape[0]):
        at = slot_ref[s]
        tile = shares_ref[jnp.maximum(at, 0)]
        picked_ref[s] = jnp.where(at >= 0, tile, jnp.zeros_like(tile))


def owner_kernel(
    own_ref, other_ref, left_stats_ref, right_stats_ref, left_root_ref, right_root_ref,
    direction_ref, left_ref, right_ref, blocks_ref, columns_ref,
):
    groups, near, slots = own_ref.shape[:3]
    order = blocks_ref.shape[1]
    band = left_ref.shape[1]
    core = lax.axis_index("core")
    me = lax.axis_index("x") * 2 + core
    my_rows = pl.ds(pl.multiple_of(me * band, band), band)
    for k in range(slots):
        for j in range(near):
            for c in range(groups):
                lanes = pl.ds(c * LANES, LANES)
                for half, ref in ((core, own_ref), (1 - core, other_ref)):
                    start = pl.multiple_of(j * 2 * TILE_ROWS + half * TILE_ROWS, TILE_ROWS)
                    blocks_ref[k, pl.ds(start, TILE_ROWS), lanes] = ref[c, j, k]
        block = blocks_ref[k]
        mine = blocks_ref[k, my_rows, :]
        left = lax.dot_general(mine, block, (((1,), (1,)), ((), ())), preferred_element_type=jnp.float32)
        left_ref[k] = 0.8 * left_stats_ref[k] + (0.2 / order) * left
        start = pl.multiple_of((me * band // LANES) * LANES, LANES)
        two_bands = blocks_ref[k, :, pl.ds(start, LANES)]
        columns_ref[...] = lax.dot_general(
            two_bands, block, (((0,), (0,)), ((), ())), preferred_element_type=jnp.float32
        )
        right = columns_ref[pl.ds(pl.multiple_of(me * band - start, band), band), :]
        right_ref[k] = 0.8 * right_stats_ref[k] + (0.2 / order) * right
        mixed = jnp.dot(block, right_root_ref[k], preferred_element_type=jnp.float32).astype(jnp.bfloat16)
        direction_ref[k] = jnp.dot(
            left_root_ref[k, my_rows, :], mixed, preferred_element_type=jnp.float32
        ).astype(jnp.bfloat16)


def per_device(
    replica_grads, block_row, block_col, block_owner, left_stats, right_stats, left_root, right_root
):
    slots, order, _ = left_root.shape
    band = left_stats.shape[1]
    local_rows, cols = replica_grads.shape[1:]
    ncb = cols // order
    groups = lax.axis_size("x")
    replicas = groups * lax.axis_size("core")
    near = lax.axis_size("zl") * lax.axis_size("y")
    cubes = lax.axis_size("cube")
    bf16 = jnp.bfloat16
    smem = pl.BlockSpec(memory_space=pltpu.SMEM)

    parts, slot = pl.pallas_call(
        lambda *refs: cut_kernel(*refs, near=near, slots=slots, ncb=ncb),
        out_shape=(
            jax.ShapeDtypeStruct((replicas, ncb, TILE_ROWS, LANES), bf16),
            jax.ShapeDtypeStruct((near * slots,), jnp.int32),
        ),
        in_specs=[smem] * 3 + vmem(1),
        out_specs=(vmem(1)[0], smem),
        scratch_shapes=[pltpu.SMEM((near,), jnp.int32)],
        name="cut",
    )(block_owner, block_row, block_col, replica_grads)

    received = lax.all_to_all(parts, ("x", "core"), 0, 0, tiled=True)
    summed = jnp.sum(received.astype(jnp.float32), axis=0).astype(bf16)
    shares = lax.all_gather(summed, "cube", axis=0, tiled=True)

    picked = pl.pallas_call(
        pick_kernel,
        out_shape=jax.ShapeDtypeStruct((near * slots, TILE_ROWS, LANES), bf16),
        in_specs=[smem] + vmem(1),
        out_specs=vmem(1)[0],
        name="pick",
    )(slot, shares)

    picked = picked.reshape(near, slots, TILE_ROWS, LANES)
    held = lax.all_to_all(picked, NEAR, 0, 0, tiled=True)
    own = lax.all_gather(held, "x", axis=0, tiled=False)
    other = lax.ppermute(own, "core", [(0, 1), (1, 0)])

    return pl.pallas_call(
        owner_kernel,
        out_shape=(
            jax.ShapeDtypeStruct((slots, band, order), bf16),
            jax.ShapeDtypeStruct((slots, band, order), jnp.float32),
            jax.ShapeDtypeStruct((slots, band, order), jnp.float32),
        ),
        in_specs=vmem(6),
        out_specs=tuple(vmem(3)),
        scratch_shapes=[
            pltpu.VMEM((slots, order, order), bf16),
            pltpu.VMEM((LANES, order), jnp.float32),
        ],
        compiler_params=pltpu.CompilerParams(vmem_limit_bytes=32 * 1024 * 1024),
        name="owner",
    )(own, other, left_stats, right_stats, left_root, right_root)


def solution(mesh):
    fine = Mesh(mesh.devices.reshape(8, 4, 4, 4, 2), ("cube", "zl", "y", "x", "core"))
    shard, replica = ("cube", "zl", "y"), ("x", "core")
    in_specs = (
        P(replica, shard, None),
        P(),
        P(),
        P(),
        P(shard, replica, None),
        P(shard, replica, None),
        P(shard, None, None),
        P(shard, None, None),
    )
    out_specs = (P(shard, replica, None),) * 3
    return jax.shard_map(
        per_device, mesh=fine, in_specs=in_specs, out_specs=out_specs, check_vma=False
    )
```

```python
import jax
import jax.numpy as jnp
from jax import lax
from jax.experimental import pallas as pl
from jax.experimental.pallas import tpu as pltpu
from jax.sharding import Mesh, PartitionSpec as P

TILE_ROWS = 16
LANES = 128


def vmem(n):
    return [pl.BlockSpec(memory_space=pltpu.VMEM)] * n


def cut_kernel(
    owner_hbm, row_hbm, col_hbm, grads_hbm, parts_ref, slot_ref,
    owner_ref, row_ref, col_ref, grads_ref, count_ref, table_sem, grads_sem, *, near, slots, ncb,
):
    grads_copy = pltpu.make_async_copy(grads_hbm, grads_ref, grads_sem)
    grads_copy.start()
    table_copies = [
        pltpu.make_async_copy(source, target, table_sem.at[i])
        for i, (source, target) in enumerate(((owner_hbm, owner_ref), (row_hbm, row_ref), (col_hbm, col_ref)))
    ]
    for copy in table_copies:
        copy.start()
    for i in range(near * slots):
        slot_ref[i] = -1
    for i in range(near):
        count_ref[i] = 0
    base = lax.axis_index("cube") * near
    for copy in table_copies:
        copy.wait()

    def put(b, carry):
        local = owner_ref[b] - base

        @pl.when((local >= 0) & (local < near))
        def _():
            rank = count_ref[local]
            slot_ref[local * slots + rank] = row_ref[b] * ncb + col_ref[b]
            count_ref[local] = rank + 1

        return carry

    lax.fori_loop(0, owner_ref.shape[0], put, 0, unroll=8)
    grads_copy.wait()
    order = grads_ref.shape[2] // ncb
    groups = order // LANES
    halves = grads_ref.shape[1] // TILE_ROWS
    for group in range(groups):
        for half in range(halves):
            for b in range(ncb):
                parts_ref[group * halves + half, b] = grads_ref[
                    0, pl.ds(half * TILE_ROWS, TILE_ROWS), pl.ds(b * order + group * LANES, LANES)
                ]


def pick_kernel(slot_ref, shares_ref, picked_ref):
    near, groups, slots = picked_ref.shape[:3]
    for o in range(near):
        for k in range(slots):
            at = slot_ref[o * slots + k]
            tile = shares_ref[jnp.maximum(at, 0)]
            tile = jnp.where(at >= 0, tile, jnp.zeros_like(tile))
            for x in range(groups):
                picked_ref[o, x, k] = tile


def owner_kernel(
    own_ref, other_ref, left_stats_ref, right_stats_ref, left_root_ref, right_root_ref,
    direction_ref, left_ref, right_ref, blocks_ref, columns_ref,
):
    near, groups, slots = own_ref.shape[:3]
    order = blocks_ref.shape[1]
    band = left_ref.shape[1]
    core = lax.axis_index("core")
    me = lax.axis_index("x") * 2 + core
    my_rows = pl.ds(pl.multiple_of(me * band, band), band)
    for k in range(slots):
        for j in range(near):
            for c in range(groups):
                lanes = pl.ds(c * LANES, LANES)
                for half, ref in ((core, own_ref), (1 - core, other_ref)):
                    start = pl.multiple_of(j * 2 * TILE_ROWS + half * TILE_ROWS, TILE_ROWS)
                    blocks_ref[k, pl.ds(start, TILE_ROWS), lanes] = ref[j, c, k]
        block = blocks_ref[k]
        mine = blocks_ref[k, my_rows, :]
        left = lax.dot_general(mine, block, (((1,), (1,)), ((), ())), preferred_element_type=jnp.float32)
        left_ref[k] = 0.8 * left_stats_ref[k] + (0.2 / order) * left
        start = pl.multiple_of((me * band // LANES) * LANES, LANES)
        two_bands = blocks_ref[k, :, pl.ds(start, LANES)]
        columns_ref[...] = lax.dot_general(
            two_bands, block, (((0,), (0,)), ((), ())), preferred_element_type=jnp.float32
        )
        right = columns_ref[pl.ds(pl.multiple_of(me * band - start, band), band), :]
        right_ref[k] = 0.8 * right_stats_ref[k] + (0.2 / order) * right
        mixed = jnp.dot(block, right_root_ref[k], preferred_element_type=jnp.float32).astype(jnp.bfloat16)
        direction_ref[k] = jnp.dot(
            left_root_ref[k, my_rows, :], mixed, preferred_element_type=jnp.float32
        ).astype(jnp.bfloat16)


def per_device(
    replica_grads, block_row, block_col, block_owner, left_stats, right_stats, left_root, right_root
):
    slots, order, _ = left_root.shape
    band = left_stats.shape[1]
    local_rows, cols = replica_grads.shape[1:]
    ncb = cols // order
    groups = lax.axis_size("x")
    replicas = groups * lax.axis_size("core")
    near = lax.axis_size("zl") * lax.axis_size("y")
    cubes = lax.axis_size("cube")
    bf16 = jnp.bfloat16
    smem = pl.BlockSpec(memory_space=pltpu.SMEM)

    parts, slot = pl.pallas_call(
        lambda *refs: cut_kernel(*refs, near=near, slots=slots, ncb=ncb),
        out_shape=(
            jax.ShapeDtypeStruct((replicas, ncb, TILE_ROWS, LANES), bf16),
            jax.ShapeDtypeStruct((near * slots,), jnp.int32),
        ),
        in_specs=[pl.BlockSpec(memory_space=pl.ANY)] * 4,
        out_specs=(vmem(1)[0], smem),
        scratch_shapes=[pltpu.SMEM(block_owner.shape, jnp.int32)] * 3
        + [
            pltpu.VMEM(replica_grads.shape, bf16),
            pltpu.SMEM((near,), jnp.int32),
            pltpu.SemaphoreType.DMA((3,)),
            pltpu.SemaphoreType.DMA,
        ],
        name="cut",
    )(block_owner, block_row, block_col, replica_grads)

    received = lax.all_to_all(parts, ("x", "core"), 0, 0, tiled=True)
    summed = jnp.sum(received.astype(jnp.float32), axis=0).astype(bf16)
    shares = lax.all_gather(summed, "cube", axis=0, tiled=True)

    picked = pl.pallas_call(
        pick_kernel,
        out_shape=jax.ShapeDtypeStruct((near, groups, slots, TILE_ROWS, LANES), bf16),
        in_specs=[smem] + vmem(1),
        out_specs=vmem(1)[0],
        name="pick",
    )(slot, shares)

    picked = picked.reshape(near * groups, slots, TILE_ROWS, LANES)
    own = lax.all_to_all(picked, ("zl", "y", "x"), 0, 0, tiled=True)
    own = own.reshape(near, groups, slots, TILE_ROWS, LANES)
    other = lax.ppermute(own, "core", [(0, 1), (1, 0)])

    return pl.pallas_call(
        owner_kernel,
        out_shape=(
            jax.ShapeDtypeStruct((slots, band, order), bf16),
            jax.ShapeDtypeStruct((slots, band, order), jnp.float32),
            jax.ShapeDtypeStruct((slots, band, order), jnp.float32),
        ),
        in_specs=vmem(6),
        out_specs=tuple(vmem(3)),
        scratch_shapes=[
            pltpu.VMEM((slots, order, order), bf16),
            pltpu.VMEM((LANES, order), jnp.float32),
        ],
        compiler_params=pltpu.CompilerParams(vmem_limit_bytes=32 * 1024 * 1024),
        name="owner",
    )(own, other, left_stats, right_stats, left_root, right_root)


def solution(mesh):
    fine = Mesh(mesh.devices.reshape(8, 4, 4, 4, 2), ("cube", "zl", "y", "x", "core"))
    shard, replica = ("cube", "zl", "y"), ("x", "core")
    in_specs = (
        P(replica, shard, None),
        P(),
        P(),
        P(),
        P(shard, replica, None),
        P(shard, replica, None),
        P(shard, None, None),
        P(shard, None, None),
    )
    out_specs = (P(shard, replica, None),) * 3
    return jax.shard_map(
        per_device, mesh=fine, in_specs=in_specs, out_specs=out_specs, check_vma=False
    )
```

```python
import functools

import jax
import jax.numpy as jnp
from jax import lax
from jax.experimental import pallas as pl
from jax.experimental.pallas import tpu as pltpu
from jax.sharding import Mesh, PartitionSpec as P

TILE_ROWS = 16
LANES = 128


def vmem(n):
    return [pl.BlockSpec(memory_space=pltpu.VMEM)] * n


def cut_kernel(
    owner_hbm, row_hbm, col_hbm, grads_hbm, parts_ref, slot_ref,
    owner_ref, row_ref, col_ref, grads_ref, count_ref, table_sem, grads_sem, *, near, slots, ncb,
):
    grads_copy = pltpu.make_async_copy(grads_hbm, grads_ref, grads_sem)
    grads_copy.start()
    table_copies = [
        pltpu.make_async_copy(source, target, table_sem.at[i])
        for i, (source, target) in enumerate(((owner_hbm, owner_ref), (row_hbm, row_ref), (col_hbm, col_ref)))
    ]
    for copy in table_copies:
        copy.start()
    halves = grads_ref.shape[1] // TILE_ROWS
    for i in range(near * slots):
        slot_ref[i] = -1
    for i in range(near):
        count_ref[i] = 0
    base = lax.axis_index("cube") * near
    for copy in table_copies:
        copy.wait()

    def put(b, carry):
        local = owner_ref[b] - base

        @pl.when((local >= 0) & (local < near))
        def _():
            rank = count_ref[local]
            slot_ref[local * slots + rank] = row_ref[b] * (halves * ncb) + col_ref[b]
            count_ref[local] = rank + 1

        return carry

    lax.fori_loop(0, owner_ref.shape[0], put, 0, unroll=8)
    grads_copy.wait()
    order = grads_ref.shape[2] // ncb
    groups = order // LANES
    for group in range(groups):
        for half in range(halves):
            for b in range(ncb):
                parts_ref[group * halves + half, b] = grads_ref[
                    0, pl.ds(half * TILE_ROWS, TILE_ROWS), pl.ds(b * order + group * LANES, LANES)
                ]


def pick_kernel(slot_ref, shares_ref, picked_ref, *, ncb):
    near, groups, halves = picked_ref.shape[:3]
    core = lax.axis_index("core")
    for o in range(near):
        at = slot_ref[o * 2 + core]
        for half in range(halves):
            tile = shares_ref[jnp.maximum(at, 0) + half * ncb]
            tile = jnp.where(at >= 0, tile, jnp.zeros_like(tile))
            for x in range(groups):
                picked_ref[o, x, half] = tile


def owner_kernel(
    own_ref, other_ref, left_stats_ref, right_stats_ref, left_root_ref, right_root_ref,
    direction_ref, left_ref, right_ref, blocks_ref, columns_ref,
):
    near, groups, halves = own_ref.shape[:3]
    order = blocks_ref.shape[1]
    band = left_ref.shape[1]
    core = lax.axis_index("core")
    me = lax.axis_index("x") * 2 + core
    my_rows = pl.ds(pl.multiple_of(me * band, band), band)
    for k, tiles_ref in ((core, own_ref), (1 - core, other_ref)):
        block_ref = blocks_ref.at[k]
        for j in range(near):
            for c in range(groups):
                for half in range(halves):
                    rows = pl.ds((j * halves + half) * TILE_ROWS, TILE_ROWS)
                    block_ref[rows, pl.ds(c * LANES, LANES)] = tiles_ref[j, c, half]
        block = block_ref[...]
        mine = block_ref[my_rows, :]
        left = lax.dot_general(mine, block, (((1,), (1,)), ((), ())), preferred_element_type=jnp.float32)
        left_ref[k] = 0.8 * left_stats_ref[k] + (0.2 / order) * left
        start = pl.multiple_of((me * band // LANES) * LANES, LANES)
        two_bands = block_ref[:, pl.ds(start, LANES)]
        columns_ref[...] = lax.dot_general(
            two_bands, block, (((0,), (0,)), ((), ())), preferred_element_type=jnp.float32
        )
        right = columns_ref[pl.ds(pl.multiple_of(me * band - start, band), band), :]
        right_ref[k] = 0.8 * right_stats_ref[k] + (0.2 / order) * right
        mixed = jnp.dot(block, right_root_ref[k], preferred_element_type=jnp.float32).astype(jnp.bfloat16)
        direction_ref[k] = jnp.dot(
            left_root_ref[k, my_rows, :], mixed, preferred_element_type=jnp.float32
        ).astype(jnp.bfloat16)


def per_device(
    replica_grads, block_row, block_col, block_owner, left_stats, right_stats, left_root, right_root
):
    slots, order, _ = left_root.shape
    band = left_stats.shape[1]
    local_rows, cols = replica_grads.shape[1:]
    ncb = cols // order
    groups, halves = lax.axis_size("x"), lax.axis_size("core")
    replicas = groups * halves
    near = lax.axis_size("zl") * lax.axis_size("y")
    cubes = lax.axis_size("cube")
    bf16 = jnp.bfloat16
    smem = pl.BlockSpec(memory_space=pltpu.SMEM)

    parts, slot = pl.pallas_call(
        functools.partial(cut_kernel, near=near, slots=slots, ncb=ncb),
        out_shape=(
            jax.ShapeDtypeStruct((replicas, ncb, TILE_ROWS, LANES), bf16),
            jax.ShapeDtypeStruct((near * slots,), jnp.int32),
        ),
        in_specs=[pl.BlockSpec(memory_space=pl.ANY)] * 4,
        out_specs=(vmem(1)[0], smem),
        scratch_shapes=[pltpu.SMEM(block_owner.shape, jnp.int32)] * 3
        + [
            pltpu.VMEM(replica_grads.shape, bf16),
            pltpu.SMEM((near,), jnp.int32),
            pltpu.SemaphoreType.DMA((3,)),
            pltpu.SemaphoreType.DMA,
        ],
        name="cut",
    )(block_owner, block_row, block_col, replica_grads)

    received = lax.all_to_all(parts, ("x", "core"), 0, 0, tiled=True)
    summed = jnp.sum(received.astype(jnp.float32), axis=0).astype(bf16)
    shares = lax.all_gather(summed, ("cube", "core"), axis=0, tiled=True)

    picked = pl.pallas_call(
        functools.partial(pick_kernel, ncb=ncb),
        out_shape=jax.ShapeDtypeStruct((near, groups, halves, TILE_ROWS, LANES), bf16),
        in_specs=[smem] + vmem(1),
        out_specs=vmem(1)[0],
        name="pick",
    )(slot, shares)

    picked = picked.reshape(near * groups, halves, TILE_ROWS, LANES)
    own = lax.all_to_all(picked, ("zl", "y", "x"), 0, 0, tiled=True)
    own = own.reshape(near, groups, halves, TILE_ROWS, LANES)
    other = lax.ppermute(own, "core", [(0, 1), (1, 0)])

    return pl.pallas_call(
        owner_kernel,
        out_shape=(
            jax.ShapeDtypeStruct((slots, band, order), bf16),
            jax.ShapeDtypeStruct((slots, band, order), jnp.float32),
            jax.ShapeDtypeStruct((slots, band, order), jnp.float32),
        ),
        in_specs=vmem(6),
        out_specs=tuple(vmem(3)),
        scratch_shapes=[
            pltpu.VMEM((slots, order, order), bf16),
            pltpu.VMEM((LANES, order), jnp.float32),
        ],
        compiler_params=pltpu.CompilerParams(vmem_limit_bytes=32 * 1024 * 1024),
        name="owner",
    )(own, other, left_stats, right_stats, left_root, right_root)


def solution(mesh):
    fine = Mesh(mesh.devices.reshape(8, 4, 4, 4, 2), ("cube", "zl", "y", "x", "core"))
    shard, replica = ("cube", "zl", "y"), ("x", "core")
    in_specs = (
        P(replica, shard, None),
        P(),
        P(),
        P(),
        P(shard, replica, None),
        P(shard, replica, None),
        P(shard, None, None),
        P(shard, None, None),
    )
    out_specs = (P(shard, replica, None),) * 3
    return jax.shard_map(
        per_device, mesh=fine, in_specs=in_specs, out_specs=out_specs, check_vma=False
    )
```

```python
import functools

import jax
import jax.numpy as jnp
from jax import lax
from jax.experimental import pallas as pl
from jax.experimental.pallas import tpu as pltpu
from jax.sharding import Mesh, PartitionSpec as P

TILE_ROWS = 16
LANES = 128


def vmem(n):
    return [pl.BlockSpec(memory_space=pltpu.VMEM)] * n


def cut_kernel(
    owner_hbm, row_hbm, col_hbm, grads_hbm, parts_ref, slot_ref,
    owner_ref, row_ref, col_ref, grads_ref, count_ref, table_sem, grads_sem, *, near, slots, ncb,
):
    grads_copy = pltpu.make_async_copy(grads_hbm, grads_ref, grads_sem)
    grads_copy.start()
    table_copies = [
        pltpu.make_async_copy(source, target, table_sem.at[i])
        for i, (source, target) in enumerate(((owner_hbm, owner_ref), (row_hbm, row_ref), (col_hbm, col_ref)))
    ]
    for copy in table_copies:
        copy.start()
    halves = grads_ref.shape[1] // TILE_ROWS
    for i in range(near * slots):
        slot_ref[i] = -1
    for i in range(near):
        count_ref[i] = 0
    base = lax.axis_index("cube") * near
    for copy in table_copies:
        copy.wait()

    def put(b, carry):
        local = owner_ref[b] - base

        @pl.when((local >= 0) & (local < near))
        def _():
            rank = count_ref[local]
            slot_ref[local * slots + rank] = row_ref[b] * (halves * ncb) + col_ref[b]
            count_ref[local] = rank + 1

        return carry

    lax.fori_loop(0, owner_ref.shape[0], put, 0, unroll=8)
    grads_copy.wait()
    order = grads_ref.shape[2] // ncb
    groups = order // LANES
    for group in range(groups):
        for half in range(halves):
            for b in range(ncb):
                parts_ref[group * halves + half, b] = grads_ref[
                    0, pl.ds(half * TILE_ROWS, TILE_ROWS), pl.ds(b * order + group * LANES, LANES)
                ]


def pick_kernel(slot_ref, shares_ref, picked_ref, *, ncb):
    near, groups, halves = picked_ref.shape[:3]
    core = lax.axis_index("core")
    for o in range(near):
        at = slot_ref[o * 2 + core]
        for half in range(halves):
            tile = shares_ref[jnp.maximum(at, 0) + half * ncb]
            tile = jnp.where(at >= 0, tile, jnp.zeros_like(tile))
            for x in range(groups):
                picked_ref[o, x, half] = tile


def owner_kernel(*refs, mine):
    if mine:
        tiles_ref, *sources, direction_hbm, left_hbm, right_hbm, stats_ref, roots_ref, right_root_ref = refs[:11]
        own_stats, own_roots, own_right_root, copy_sem = refs[11:15]
    else:
        tiles_ref, own_stats, own_roots, own_right_root, _, _, _, direction_hbm, left_hbm, right_hbm = refs[:10]
    block_ref, columns_ref, direction_ref, left_ref, right_ref, out_sem = refs[-6:]
    near, groups, halves = tiles_ref.shape[:3]
    order = block_ref.shape[0]
    band = left_ref.shape[0]
    core = lax.axis_index("core")
    me = lax.axis_index("x") * 2 + core
    k = core if mine else 1 - core
    my_rows = pl.ds(pl.multiple_of(me * band, band), band)
    copies = []
    if mine:
        left_stats, right_stats, left_root, right_root = sources
        moves = [
            (left_stats.at[k], own_stats.at[0]),
            (right_stats.at[k], own_stats.at[1]),
            (left_root.at[k, my_rows, :], own_roots),
            (right_root.at[k], own_right_root),
            (left_stats.at[1 - k], stats_ref.at[0]),
            (right_stats.at[1 - k], stats_ref.at[1]),
            (left_root.at[1 - k, my_rows, :], roots_ref),
            (right_root.at[1 - k], right_root_ref),
        ]
        copies = [pltpu.make_async_copy(src, dst, copy_sem.at[i]) for i, (src, dst) in enumerate(moves)]
        for copy in copies:
            copy.start()
    for j in range(near):
        for c in range(groups):
            for half in range(halves):
                rows = pl.ds((j * halves + half) * TILE_ROWS, TILE_ROWS)
                block_ref[rows, pl.ds(c * LANES, LANES)] = tiles_ref[j, c, half]
    block = block_ref[...]
    results = [
        pltpu.make_async_copy(src, dst.at[k], out_sem.at[i])
        for i, (src, dst) in enumerate(
            ((left_ref, left_hbm), (right_ref, right_hbm), (direction_ref, direction_hbm))
        )
    ]
    for copy in copies[:4]:
        copy.wait()
    rows = block_ref[my_rows, :]
    left = lax.dot_general(rows, block, (((1,), (1,)), ((), ())), preferred_element_type=jnp.float32)
    left_ref[...] = 0.8 * own_stats[0] + (0.2 / order) * left
    results[0].start()
    start = pl.multiple_of((me * band // LANES) * LANES, LANES)
    two_bands = block_ref[:, pl.ds(start, LANES)]
    columns_ref[...] = lax.dot_general(
        two_bands, block, (((0,), (0,)), ((), ())), preferred_element_type=jnp.float32
    )
    right = columns_ref[pl.ds(pl.multiple_of(me * band - start, band), band), :]
    right_ref[...] = 0.8 * own_stats[1] + (0.2 / order) * right
    results[1].start()
    mixed = jnp.dot(block, own_right_root[...], preferred_element_type=jnp.float32).astype(jnp.bfloat16)
    direction_ref[...] = jnp.dot(
        own_roots[...], mixed, preferred_element_type=jnp.float32
    ).astype(jnp.bfloat16)
    results[2].start()
    for copy in copies[4:] + results:
        copy.wait()


def owner_call(mine, operands, slots, band, order):
    bf16, f32 = jnp.bfloat16, jnp.float32
    hbm = pl.BlockSpec(memory_space=pl.ANY)
    shapes = ((2, band, order), f32), ((band, order), bf16), ((order, order), bf16)
    outs = tuple(jax.ShapeDtypeStruct((slots, band, order), t) for t in (bf16, f32, f32))
    if mine:
        in_specs = vmem(1) + [hbm] * 4
        out_shape = outs + tuple(pltpu.VMEM(*shape) for shape in shapes)
        out_specs = (hbm,) * 3 + tuple(vmem(3))
        scratch = [pltpu.VMEM(*shape) for shape in shapes] + [pltpu.SemaphoreType.DMA((8,))]
        aliases = {}
    else:
        in_specs = vmem(4) + [hbm] * 3
        out_shape = outs
        out_specs = (hbm,) * 3
        scratch = []
        aliases = {4: 0, 5: 1, 6: 2}
    scratch += [
        pltpu.VMEM((order, order), bf16),
        pltpu.VMEM((LANES, order), f32),
        pltpu.VMEM((band, order), bf16),
        pltpu.VMEM((band, order), f32),
        pltpu.VMEM((band, order), f32),
        pltpu.SemaphoreType.DMA((3,)),
    ]
    return pl.pallas_call(
        functools.partial(owner_kernel, mine=mine),
        out_shape=out_shape,
        in_specs=in_specs,
        out_specs=out_specs,
        scratch_shapes=scratch,
        input_output_aliases=aliases,
        compiler_params=pltpu.CompilerParams(vmem_limit_bytes=32 * 1024 * 1024),
        cost_estimate=pl.CostEstimate(
            flops=2 * order * order * (order + 4 * band), bytes_accessed=8 * order * order, transcendentals=0
        ),
        name="own" if mine else "other",
    )(*operands)


def per_device(
    replica_grads, block_row, block_col, block_owner, left_stats, right_stats, left_root, right_root
):
    slots, order, _ = left_root.shape
    band = left_stats.shape[1]
    local_rows, cols = replica_grads.shape[1:]
    ncb = cols // order
    groups, halves = lax.axis_size("x"), lax.axis_size("core")
    replicas = groups * halves
    near = lax.axis_size("zl") * lax.axis_size("y")
    cubes = lax.axis_size("cube")
    bf16 = jnp.bfloat16
    smem = pl.BlockSpec(memory_space=pltpu.SMEM)

    parts, slot = pl.pallas_call(
        functools.partial(cut_kernel, near=near, slots=slots, ncb=ncb),
        out_shape=(
            pltpu.VMEM((replicas, ncb, TILE_ROWS, LANES), bf16),
            jax.ShapeDtypeStruct((near * slots,), jnp.int32),
        ),
        in_specs=[pl.BlockSpec(memory_space=pl.ANY)] * 4,
        out_specs=(vmem(1)[0], smem),
        scratch_shapes=[pltpu.SMEM(block_owner.shape, jnp.int32)] * 3
        + [
            pltpu.VMEM(replica_grads.shape, bf16),
            pltpu.SMEM((near,), jnp.int32),
            pltpu.SemaphoreType.DMA((3,)),
            pltpu.SemaphoreType.DMA,
        ],
        name="cut",
    )(block_owner, block_row, block_col, replica_grads)

    received = lax.all_to_all(parts, ("x", "core"), 0, 0, tiled=True)
    summed = jnp.sum(received.astype(jnp.float32), axis=0).astype(bf16)
    shares = lax.all_gather(summed, ("cube", "core"), axis=0, tiled=True)
    shares = pltpu.with_memory_space_constraint(shares, pltpu.VMEM)

    picked = pl.pallas_call(
        functools.partial(pick_kernel, ncb=ncb),
        out_shape=pltpu.VMEM((near, groups, halves, TILE_ROWS, LANES), bf16),
        in_specs=[smem] + vmem(1),
        out_specs=vmem(1)[0],
        name="pick",
    )(slot, shares)

    picked = picked.reshape(near * groups, halves, TILE_ROWS, LANES)
    own = lax.all_to_all(picked, ("zl", "y", "x"), 0, 0, tiled=True)
    own = own.reshape(near, groups, halves, TILE_ROWS, LANES)
    other = lax.ppermute(own, "core", [(0, 1), (1, 0)])

    operands = own, left_stats, right_stats, left_root, right_root
    *results, stats, roots, right = owner_call(True, operands, slots, band, order)
    return owner_call(False, (other, stats, roots, right, *results), slots, band, order)


def solution(mesh):
    fine = Mesh(mesh.devices.reshape(8, 4, 4, 4, 2), ("cube", "zl", "y", "x", "core"))
    shard, replica = ("cube", "zl", "y"), ("x", "core")
    in_specs = (
        P(replica, shard, None),
        P(),
        P(),
        P(),
        P(shard, replica, None),
        P(shard, replica, None),
        P(shard, None, None),
        P(shard, None, None),
    )
    out_specs = (P(shard, replica, None),) * 3
    return jax.shard_map(
        per_device, mesh=fine, in_specs=in_specs, out_specs=out_specs, check_vma=False
    )
```

```python
import functools

import jax
import jax.numpy as jnp
from jax import lax
from jax.experimental import pallas as pl
from jax.experimental.pallas import tpu as pltpu
from jax.sharding import Mesh, PartitionSpec as P

TILE_ROWS = 16
LANES = 128


def vmem(n):
    return [pl.BlockSpec(memory_space=pltpu.VMEM)] * n


def cut_kernel(
    owner_hbm, row_hbm, col_hbm, grads_hbm, parts_ref, slot_ref,
    owner_ref, row_ref, col_ref, grads_ref, count_ref, table_sem, grads_sem, *, near, slots, ncb,
):
    grads_copy = pltpu.make_async_copy(grads_hbm, grads_ref, grads_sem)
    grads_copy.start()
    table_copies = [
        pltpu.make_async_copy(source, target, table_sem.at[i])
        for i, (source, target) in enumerate(((owner_hbm, owner_ref), (row_hbm, row_ref), (col_hbm, col_ref)))
    ]
    for copy in table_copies:
        copy.start()
    halves = grads_ref.shape[1] // TILE_ROWS
    for i in range(near * slots):
        slot_ref[i] = -1
    for i in range(near):
        count_ref[i] = 0
    base = lax.axis_index("cube") * near
    for copy in table_copies:
        copy.wait()

    def put(b, carry):
        local = owner_ref[b] - base

        @pl.when((local >= 0) & (local < near))
        def _():
            rank = count_ref[local]
            slot_ref[local * slots + rank] = row_ref[b] * (halves * ncb) + col_ref[b]
            count_ref[local] = rank + 1

        return carry

    lax.fori_loop(0, owner_ref.shape[0], put, 0, unroll=8)
    grads_copy.wait()
    order = grads_ref.shape[2] // ncb
    groups = order // LANES
    for group in range(groups):
        for half in range(halves):
            for b in range(ncb):
                parts_ref[group * halves + half, b] = grads_ref[
                    0, pl.ds(half * TILE_ROWS, TILE_ROWS), pl.ds(b * order + group * LANES, LANES)
                ]


def pick_kernel(slot_ref, shares_ref, picked_ref, *, ncb):
    near, groups, halves = picked_ref.shape[:3]
    core = lax.axis_index("core")
    for o in range(near):
        at = slot_ref[o * 2 + core]
        for half in range(halves):
            tile = shares_ref[jnp.maximum(at, 0) + half * ncb]
            tile = jnp.where(at >= 0, tile, jnp.zeros_like(tile))
            for x in range(groups):
                picked_ref[o, x, half] = tile


def owner_kernel(
    tiles_ref, left_stats_ref, right_stats_ref, left_root_ref, right_root_ref, *refs, mine
):
    if mine:
        direction_hbm, left_hbm, right_hbm, staged_ref, stats_ref, stats_sem = refs[:6]
    else:
        direction_hbm, left_hbm, right_hbm = refs[3:6]
        stats_ref = right_stats_ref
    block_ref, columns_ref, direction_ref, left_ref, right_ref, out_sem = refs[-6:]
    near, groups, halves = tiles_ref.shape[:3]
    order = block_ref.shape[0]
    band = left_ref.shape[0]
    core = lax.axis_index("core")
    me = lax.axis_index("x") * 2 + core
    k = core if mine else 1 - core
    my_rows = pl.ds(pl.multiple_of(me * band, band), band)
    copies = []
    if mine:
        copies = [
            pltpu.make_async_copy(right_stats_ref.at[k], stats_ref, stats_sem.at[0]),
            pltpu.make_async_copy(right_stats_ref.at[1 - k], staged_ref, stats_sem.at[1]),
        ]
        for copy in copies:
            copy.start()
    for j in range(near):
        for c in range(groups):
            for half in range(halves):
                rows = pl.ds((j * halves + half) * TILE_ROWS, TILE_ROWS)
                block_ref[rows, pl.ds(c * LANES, LANES)] = tiles_ref[j, c, half]
    block = block_ref[...]
    results = [
        pltpu.make_async_copy(src, dst.at[k], out_sem.at[i])
        for i, (src, dst) in enumerate(
            ((left_ref, left_hbm), (right_ref, right_hbm), (direction_ref, direction_hbm))
        )
    ]
    rows = block_ref[my_rows, :]
    left = lax.dot_general(rows, block, (((1,), (1,)), ((), ())), preferred_element_type=jnp.float32)
    left_ref[...] = 0.8 * left_stats_ref[k] + (0.2 / order) * left
    results[0].start()
    start = pl.multiple_of((me * band // LANES) * LANES, LANES)
    two_bands = block_ref[:, pl.ds(start, LANES)]
    columns_ref[...] = lax.dot_general(
        two_bands, block, (((0,), (0,)), ((), ())), preferred_element_type=jnp.float32
    )
    right = columns_ref[pl.ds(pl.multiple_of(me * band - start, band), band), :]
    for copy in copies[:1]:
        copy.wait()
    right_ref[...] = 0.8 * stats_ref[...] + (0.2 / order) * right
    results[1].start()
    mixed = jnp.dot(block, right_root_ref[k], preferred_element_type=jnp.float32).astype(jnp.bfloat16)
    direction_ref[...] = jnp.dot(
        left_root_ref[k, my_rows, :], mixed, preferred_element_type=jnp.float32
    ).astype(jnp.bfloat16)
    results[2].start()
    for copy in copies[1:] + results:
        copy.wait()


def owner_call(mine, operands, slots, band, order):
    bf16, f32 = jnp.bfloat16, jnp.float32
    hbm = pl.BlockSpec(memory_space=pl.ANY)
    out_shape = tuple(jax.ShapeDtypeStruct((slots, band, order), t) for t in (bf16, f32, f32))
    out_specs = (hbm,) * 3
    scratch = []
    if mine:
        in_specs = vmem(2) + [hbm] + vmem(2)
        out_shape += (pltpu.VMEM((band, order), f32),)
        out_specs += tuple(vmem(1))
        scratch = [pltpu.VMEM((band, order), f32), pltpu.SemaphoreType.DMA((2,))]
        aliases = {}
    else:
        in_specs = vmem(5) + [hbm] * 3
        aliases = {5: 0, 6: 1, 7: 2}
    scratch += [
        pltpu.VMEM((order, order), bf16),
        pltpu.VMEM((LANES, order), f32),
        pltpu.VMEM((band, order), bf16),
        pltpu.VMEM((band, order), f32),
        pltpu.VMEM((band, order), f32),
        pltpu.SemaphoreType.DMA((3,)),
    ]
    return pl.pallas_call(
        functools.partial(owner_kernel, mine=mine),
        out_shape=out_shape,
        in_specs=in_specs,
        out_specs=out_specs,
        scratch_shapes=scratch,
        input_output_aliases=aliases,
        compiler_params=pltpu.CompilerParams(vmem_limit_bytes=32 * 1024 * 1024),
        cost_estimate=pl.CostEstimate(
            flops=2 * order * order * (order + 4 * band), bytes_accessed=8 * order * order, transcendentals=0
        ),
        name="own" if mine else "other",
    )(*operands)


def per_device(
    replica_grads, block_row, block_col, block_owner, left_stats, right_stats, left_root, right_root
):
    slots, order, _ = left_root.shape
    band = left_stats.shape[1]
    local_rows, cols = replica_grads.shape[1:]
    ncb = cols // order
    groups, halves = lax.axis_size("x"), lax.axis_size("core")
    replicas = groups * halves
    near = lax.axis_size("zl") * lax.axis_size("y")
    cubes = lax.axis_size("cube")
    bf16 = jnp.bfloat16
    smem = pl.BlockSpec(memory_space=pltpu.SMEM)

    parts, slot = pl.pallas_call(
        functools.partial(cut_kernel, near=near, slots=slots, ncb=ncb),
        out_shape=(
            pltpu.VMEM((replicas, ncb, TILE_ROWS, LANES), bf16),
            jax.ShapeDtypeStruct((near * slots,), jnp.int32),
        ),
        in_specs=[pl.BlockSpec(memory_space=pl.ANY)] * 4,
        out_specs=(vmem(1)[0], smem),
        scratch_shapes=[pltpu.SMEM(block_owner.shape, jnp.int32)] * 3
        + [
            pltpu.VMEM(replica_grads.shape, bf16),
            pltpu.SMEM((near,), jnp.int32),
            pltpu.SemaphoreType.DMA((3,)),
            pltpu.SemaphoreType.DMA,
        ],
        name="cut",
    )(block_owner, block_row, block_col, replica_grads)

    received = lax.all_to_all(parts, ("x", "core"), 0, 0, tiled=True)
    summed = jnp.sum(received.astype(jnp.float32), axis=0).astype(bf16)
    shares = lax.all_gather(summed, ("cube", "core"), axis=0, tiled=True)
    shares = pltpu.with_memory_space_constraint(shares, pltpu.VMEM)

    picked = pl.pallas_call(
        functools.partial(pick_kernel, ncb=ncb),
        out_shape=pltpu.VMEM((near, groups, halves, TILE_ROWS, LANES), bf16),
        in_specs=[smem] + vmem(1),
        out_specs=vmem(1)[0],
        name="pick",
    )(slot, shares)

    picked = picked.reshape(near * groups, halves, TILE_ROWS, LANES)
    own = lax.all_to_all(picked, ("zl", "y", "x"), 0, 0, tiled=True)
    own = own.reshape(near, groups, halves, TILE_ROWS, LANES)
    other = lax.ppermute(own, "core", [(0, 1), (1, 0)])

    left_stats, left_root, right_root = (
        pltpu.with_memory_space_constraint(a, pltpu.VMEM) for a in (left_stats, left_root, right_root)
    )
    right_stats = pltpu.with_memory_space_constraint(right_stats, pltpu.HBM)
    operands = own, left_stats, right_stats, left_root, right_root
    *results, staged = owner_call(True, operands, slots, band, order)
    operands = other, left_stats, staged, left_root, right_root
    return owner_call(False, (*operands, *results), slots, band, order)


def solution(mesh):
    fine = Mesh(mesh.devices.reshape(8, 4, 4, 4, 2), ("cube", "zl", "y", "x", "core"))
    shard, replica = ("cube", "zl", "y"), ("x", "core")
    in_specs = (
        P(replica, shard, None),
        P(),
        P(),
        P(),
        P(shard, replica, None),
        P(shard, replica, None),
        P(shard, None, None),
        P(shard, None, None),
    )
    out_specs = (P(shard, replica, None),) * 3
    return jax.shard_map(
        per_device, mesh=fine, in_specs=in_specs, out_specs=out_specs, check_vma=False
    )
```

```python
import functools

import jax
import jax.numpy as jnp
from jax import lax
from jax.experimental import pallas as pl
from jax.experimental.pallas import tpu as pltpu
from jax.sharding import Mesh, PartitionSpec as P

TILE_ROWS = 16
LANES = 128


def vmem(n):
    return [pl.BlockSpec(memory_space=pltpu.VMEM)] * n


def cut_kernel(
    owner_hbm, row_hbm, col_hbm, grads_hbm, stats_hbm, parts_ref, slot_ref, stats_ref,
    owner_ref, row_ref, col_ref, grads_ref, count_ref, table_sem, grads_sem, stats_sem, *, near, slots, ncb,
):
    grads_copy = pltpu.make_async_copy(grads_hbm, grads_ref, grads_sem)
    grads_copy.start()
    table_copies = [
        pltpu.make_async_copy(source, target, table_sem.at[i])
        for i, (source, target) in enumerate(((owner_hbm, owner_ref), (row_hbm, row_ref), (col_hbm, col_ref)))
    ]
    for copy in table_copies:
        copy.start()
    stats_copy = pltpu.make_async_copy(stats_hbm, stats_ref, stats_sem)
    stats_copy.start()
    halves = grads_ref.shape[1] // TILE_ROWS
    for i in range(slot_ref.shape[0]):
        slot_ref[i] = -1
    for i in range(count_ref.shape[0]):
        count_ref[i] = 0
    base = lax.axis_index("cube") * near
    for copy in table_copies:
        copy.wait()

    def put(b, carry):
        local = owner_ref[b] - base
        mine = (local >= 0) & (local < near)
        local = jnp.where(mine, local, near)
        rank = count_ref[local]
        slot_ref[local * slots + rank] = row_ref[b] * (halves * ncb) + col_ref[b]
        count_ref[local] = rank + mine.astype(jnp.int32)
        return carry

    lax.fori_loop(0, owner_ref.shape[0], put, 0, unroll=8)
    grads_copy.wait()
    order = grads_ref.shape[2] // ncb
    groups = order // LANES
    for group in range(groups):
        for half in range(halves):
            for b in range(ncb):
                parts_ref[group * halves + half, b] = grads_ref[
                    0, pl.ds(half * TILE_ROWS, TILE_ROWS), pl.ds(b * order + group * LANES, LANES)
                ]
    stats_copy.wait()


def pick_kernel(slot_ref, shares_ref, picked_ref, *, ncb):
    near, groups, halves = picked_ref.shape[:3]
    core = lax.axis_index("core")
    for o in range(near):
        at = slot_ref[o * 2 + core]
        for half in range(halves):
            tile = shares_ref[jnp.maximum(at, 0) + half * ncb]
            tile = jnp.where(at >= 0, tile, jnp.zeros_like(tile))
            for x in range(groups):
                picked_ref[o, x, half] = tile


def owner_kernel(
    tiles_ref, left_stats_ref, right_stats_ref, left_root_ref, right_root_ref, *refs, mine
):
    direction_hbm, left_hbm, right_hbm = refs[-9:-6]
    block_ref, columns_ref, direction_ref, left_ref, right_ref, out_sem = refs[-6:]
    near, groups, halves = tiles_ref.shape[:3]
    order = block_ref.shape[0]
    band = left_ref.shape[0]
    core = lax.axis_index("core")
    me = lax.axis_index("x") * 2 + core
    k = core if mine else 1 - core
    my_rows = pl.ds(pl.multiple_of(me * band, band), band)
    for j in range(near):
        for c in range(groups):
            for half in range(halves):
                rows = pl.ds((j * halves + half) * TILE_ROWS, TILE_ROWS)
                block_ref[rows, pl.ds(c * LANES, LANES)] = tiles_ref[j, c, half]
    block = block_ref[...]
    results = [
        pltpu.make_async_copy(src, dst.at[k], out_sem.at[i])
        for i, (src, dst) in enumerate(
            ((left_ref, left_hbm), (right_ref, right_hbm), (direction_ref, direction_hbm))
        )
    ]
    rows = block_ref[my_rows, :]
    left = lax.dot_general(rows, block, (((1,), (1,)), ((), ())), preferred_element_type=jnp.float32)
    left_ref[...] = 0.8 * left_stats_ref[k] + (0.2 / order) * left
    results[0].start()
    start = pl.multiple_of((me * band // LANES) * LANES, LANES)
    two_bands = block_ref[:, pl.ds(start, LANES)]
    columns_ref[...] = lax.dot_general(
        two_bands, block, (((0,), (0,)), ((), ())), preferred_element_type=jnp.float32
    )
    right = columns_ref[pl.ds(pl.multiple_of(me * band - start, band), band), :]
    right_ref[...] = 0.8 * right_stats_ref[k] + (0.2 / order) * right
    results[1].start()
    mixed = jnp.dot(block, right_root_ref[k], preferred_element_type=jnp.float32).astype(jnp.bfloat16)
    direction_ref[...] = jnp.dot(
        left_root_ref[k, my_rows, :], mixed, preferred_element_type=jnp.float32
    ).astype(jnp.bfloat16)
    results[2].start()
    for copy in results:
        copy.wait()


def owner_call(mine, operands, slots, band, order):
    bf16, f32 = jnp.bfloat16, jnp.float32
    hbm = pl.BlockSpec(memory_space=pl.ANY)
    aliases = {} if mine else {5: 0, 6: 1, 7: 2}
    scratch = [
        pltpu.VMEM((order, order), bf16),
        pltpu.VMEM((LANES, order), f32),
        pltpu.VMEM((band, order), bf16),
        pltpu.VMEM((band, order), f32),
        pltpu.VMEM((band, order), f32),
        pltpu.SemaphoreType.DMA((3,)),
    ]
    return pl.pallas_call(
        functools.partial(owner_kernel, mine=mine),
        out_shape=tuple(jax.ShapeDtypeStruct((slots, band, order), t) for t in (bf16, f32, f32)),
        in_specs=vmem(5) + [hbm] * len(aliases),
        out_specs=(hbm,) * 3,
        scratch_shapes=scratch,
        input_output_aliases=aliases,
        compiler_params=pltpu.CompilerParams(vmem_limit_bytes=32 * 1024 * 1024),
        cost_estimate=pl.CostEstimate(
            flops=2 * order * order * (order + 4 * band), bytes_accessed=8 * order * order, transcendentals=0
        ),
        name="own" if mine else "other",
    )(*operands)


def per_device(
    replica_grads, block_row, block_col, block_owner, left_stats, right_stats, left_root, right_root
):
    slots, order, _ = left_root.shape
    band = left_stats.shape[1]
    ncb = replica_grads.shape[2] // order
    groups, halves = lax.axis_size("x"), lax.axis_size("core")
    replicas = groups * halves
    near = lax.axis_size("zl") * lax.axis_size("y")
    bf16 = jnp.bfloat16
    smem = pl.BlockSpec(memory_space=pltpu.SMEM)

    parts, slot, right_stats = pl.pallas_call(
        functools.partial(cut_kernel, near=near, slots=slots, ncb=ncb),
        out_shape=(
            pltpu.VMEM((replicas, ncb, TILE_ROWS, LANES), bf16),
            jax.ShapeDtypeStruct(((near + 1) * slots,), jnp.int32),
            pltpu.VMEM(right_stats.shape, jnp.float32),
        ),
        in_specs=[pl.BlockSpec(memory_space=pl.ANY)] * 5,
        out_specs=(vmem(1)[0], smem, vmem(1)[0]),
        scratch_shapes=[pltpu.SMEM(block_owner.shape, jnp.int32)] * 3
        + [
            pltpu.VMEM(replica_grads.shape, bf16),
            pltpu.SMEM((near + 1,), jnp.int32),
            pltpu.SemaphoreType.DMA((3,)),
            pltpu.SemaphoreType.DMA,
            pltpu.SemaphoreType.DMA,
        ],
        name="cut",
    )(block_owner, block_row, block_col, replica_grads, right_stats)

    received = lax.all_to_all(parts, ("x", "core"), 0, 0, tiled=True)
    summed = jnp.sum(received.astype(jnp.float32), axis=0).astype(bf16)
    shares = lax.all_gather(summed, ("cube", "core"), axis=0, tiled=True)
    shares = pltpu.with_memory_space_constraint(shares, pltpu.VMEM)

    picked = pl.pallas_call(
        functools.partial(pick_kernel, ncb=ncb),
        out_shape=pltpu.VMEM((near, groups, halves, TILE_ROWS, LANES), bf16),
        in_specs=[smem] + vmem(1),
        out_specs=vmem(1)[0],
        name="pick",
    )(slot, shares)

    picked = picked.reshape(near * groups, halves, TILE_ROWS, LANES)
    own = lax.all_to_all(picked, ("zl", "y", "x"), 0, 0, tiled=True)
    own = own.reshape(near, groups, halves, TILE_ROWS, LANES)
    other = lax.ppermute(own, "core", [(0, 1), (1, 0)])

    left_stats, left_root, right_root = (
        pltpu.with_memory_space_constraint(a, pltpu.VMEM) for a in (left_stats, left_root, right_root)
    )
    operands = left_stats, right_stats, left_root, right_root
    results = owner_call(True, (own, *operands), slots, band, order)
    return owner_call(False, (other, *operands, *results), slots, band, order)


def solution(mesh):
    fine = Mesh(mesh.devices.reshape(8, 4, 4, 4, 2), ("cube", "zl", "y", "x", "core"))
    shard, replica = ("cube", "zl", "y"), ("x", "core")
    in_specs = (
        P(replica, shard, None),
        P(),
        P(),
        P(),
        P(shard, replica, None),
        P(shard, replica, None),
        P(shard, None, None),
        P(shard, None, None),
    )
    out_specs = (P(shard, replica, None),) * 3
    return jax.shard_map(
        per_device, mesh=fine, in_specs=in_specs, out_specs=out_specs, check_vma=False
    )
```

```python
import functools

import jax
import jax.numpy as jnp
from jax import lax
from jax.experimental import pallas as pl
from jax.experimental.pallas import tpu as pltpu
from jax.sharding import Mesh, PartitionSpec as P

TILE_ROWS = 16
LANES = 128


def vmem(n):
    return [pl.BlockSpec(memory_space=pltpu.VMEM)] * n


def cut_kernel(
    owner_hbm, row_hbm, col_hbm, grads_hbm, parts_ref, slot_ref,
    owner_ref, row_ref, col_ref, grads_ref, count_ref, table_sem, grads_sem, *, near, slots, ncb,
):
    grads_copy = pltpu.make_async_copy(grads_hbm, grads_ref, grads_sem)
    grads_copy.start()
    table_copies = [
        pltpu.make_async_copy(source, target, table_sem.at[i])
        for i, (source, target) in enumerate(((owner_hbm, owner_ref), (row_hbm, row_ref), (col_hbm, col_ref)))
    ]
    for copy in table_copies:
        copy.start()
    halves = grads_ref.shape[1] // TILE_ROWS
    for i in range(slot_ref.shape[0]):
        slot_ref[i] = -1
    for i in range(count_ref.shape[0]):
        count_ref[i] = 0
    base = lax.axis_index("cube") * near
    for copy in table_copies:
        copy.wait()

    def put(b, carry):
        local = owner_ref[b] - base
        mine = (local >= 0) & (local < near)
        local = jnp.where(mine, local, near)
        rank = count_ref[local]
        slot_ref[local * slots + rank] = row_ref[b] * (halves * ncb) + col_ref[b]
        count_ref[local] = rank + mine.astype(jnp.int32)
        return carry

    lax.fori_loop(0, owner_ref.shape[0], put, 0, unroll=8)
    grads_copy.wait()
    order = grads_ref.shape[2] // ncb
    groups = order // LANES
    for group in range(groups):
        for half in range(halves):
            for b in range(ncb):
                parts_ref[group * halves + half, b] = grads_ref[
                    0, pl.ds(half * TILE_ROWS, TILE_ROWS), pl.ds(b * order + group * LANES, LANES)
                ]


def pick_kernel(slot_ref, shares_ref, stats_hbm, picked_ref, stats_ref, stats_sem, *, ncb):
    stats_copy = pltpu.make_async_copy(stats_hbm, stats_ref, stats_sem)
    stats_copy.start()
    near, groups, halves = picked_ref.shape[:3]
    core = lax.axis_index("core")
    for o in range(near):
        at = slot_ref[o * 2 + core]
        for half in range(halves):
            tile = shares_ref[jnp.maximum(at, 0) + half * ncb]
            tile = jnp.where(at >= 0, tile, jnp.zeros_like(tile))
            for x in range(groups):
                picked_ref[o, x, half] = tile
    stats_copy.wait()


def owner_kernel(
    tiles_ref, left_stats_ref, right_stats_ref, left_root_ref, right_root_ref, *refs, mine
):
    direction_hbm, left_hbm, right_hbm = refs[-9:-6]
    block_ref, columns_ref, direction_ref, left_ref, right_ref, out_sem = refs[-6:]
    near, groups, halves = tiles_ref.shape[:3]
    order = block_ref.shape[0]
    band = left_ref.shape[0]
    core = lax.axis_index("core")
    me = lax.axis_index("x") * 2 + core
    k = core if mine else 1 - core
    my_rows = pl.ds(pl.multiple_of(me * band, band), band)
    for j in range(near):
        for c in range(groups):
            for half in range(halves):
                rows = pl.ds((j * halves + half) * TILE_ROWS, TILE_ROWS)
                block_ref[rows, pl.ds(c * LANES, LANES)] = tiles_ref[j, c, half]
    block = block_ref[...]
    results = [
        pltpu.make_async_copy(src, dst.at[k], out_sem.at[i])
        for i, (src, dst) in enumerate(
            ((left_ref, left_hbm), (right_ref, right_hbm), (direction_ref, direction_hbm))
        )
    ]
    rows = block_ref[my_rows, :]
    left = lax.dot_general(rows, block, (((1,), (1,)), ((), ())), preferred_element_type=jnp.float32)
    left_ref[...] = 0.8 * left_stats_ref[k] + (0.2 / order) * left
    results[0].start()
    start = pl.multiple_of((me * band // LANES) * LANES, LANES)
    two_bands = block_ref[:, pl.ds(start, LANES)]
    columns_ref[...] = lax.dot_general(
        two_bands, block, (((0,), (0,)), ((), ())), preferred_element_type=jnp.float32
    )
    right = columns_ref[pl.ds(pl.multiple_of(me * band - start, band), band), :]
    right_ref[...] = 0.8 * right_stats_ref[k] + (0.2 / order) * right
    results[1].start()
    mixed = jnp.dot(block, right_root_ref[k], preferred_element_type=jnp.float32).astype(jnp.bfloat16)
    direction_ref[...] = jnp.dot(
        left_root_ref[k, my_rows, :], mixed, preferred_element_type=jnp.float32
    ).astype(jnp.bfloat16)
    results[2].start()
    for copy in results:
        copy.wait()


def owner_call(mine, operands, slots, band, order):
    bf16, f32 = jnp.bfloat16, jnp.float32
    hbm = pl.BlockSpec(memory_space=pl.ANY)
    aliases = {} if mine else {5: 0, 6: 1, 7: 2}
    scratch = [
        pltpu.VMEM((order, order), bf16),
        pltpu.VMEM((LANES, order), f32),
        pltpu.VMEM((band, order), bf16),
        pltpu.VMEM((band, order), f32),
        pltpu.VMEM((band, order), f32),
        pltpu.SemaphoreType.DMA((3,)),
    ]
    return pl.pallas_call(
        functools.partial(owner_kernel, mine=mine),
        out_shape=tuple(jax.ShapeDtypeStruct((slots, band, order), t) for t in (bf16, f32, f32)),
        in_specs=vmem(5) + [hbm] * len(aliases),
        out_specs=(hbm,) * 3,
        scratch_shapes=scratch,
        input_output_aliases=aliases,
        compiler_params=pltpu.CompilerParams(vmem_limit_bytes=32 * 1024 * 1024),
        cost_estimate=pl.CostEstimate(
            flops=2 * order * order * (order + 4 * band), bytes_accessed=8 * order * order, transcendentals=0
        ),
        name="own" if mine else "other",
    )(*operands)


def per_device(
    replica_grads, block_row, block_col, block_owner, left_stats, right_stats, left_root, right_root
):
    slots, order, _ = left_root.shape
    band = left_stats.shape[1]
    ncb = replica_grads.shape[2] // order
    groups, halves = lax.axis_size("x"), lax.axis_size("core")
    replicas = groups * halves
    near = lax.axis_size("zl") * lax.axis_size("y")
    bf16 = jnp.bfloat16
    smem = pl.BlockSpec(memory_space=pltpu.SMEM)

    parts, slot = pl.pallas_call(
        functools.partial(cut_kernel, near=near, slots=slots, ncb=ncb),
        out_shape=(
            pltpu.VMEM((replicas, ncb, TILE_ROWS, LANES), bf16),
            jax.ShapeDtypeStruct(((near + 1) * slots,), jnp.int32),
        ),
        in_specs=[pl.BlockSpec(memory_space=pl.ANY)] * 4,
        out_specs=(vmem(1)[0], smem),
        scratch_shapes=[pltpu.SMEM(block_owner.shape, jnp.int32)] * 3
        + [
            pltpu.VMEM(replica_grads.shape, bf16),
            pltpu.SMEM((near + 1,), jnp.int32),
            pltpu.SemaphoreType.DMA((3,)),
            pltpu.SemaphoreType.DMA,
        ],
        name="cut",
    )(block_owner, block_row, block_col, replica_grads)

    received = lax.all_to_all(parts, ("x", "core"), 0, 0, tiled=True)
    summed = jnp.sum(received.astype(jnp.float32), axis=0).astype(bf16)
    shares = lax.all_gather(summed, ("cube", "core"), axis=0, tiled=True)
    shares = pltpu.with_memory_space_constraint(shares, pltpu.VMEM)

    picked, right_stats = pl.pallas_call(
        functools.partial(pick_kernel, ncb=ncb),
        out_shape=(
            pltpu.VMEM((near, groups, halves, TILE_ROWS, LANES), bf16),
            pltpu.VMEM(right_stats.shape, jnp.float32),
        ),
        in_specs=[smem] + vmem(1) + [pl.BlockSpec(memory_space=pl.ANY)],
        out_specs=tuple(vmem(2)),
        scratch_shapes=[pltpu.SemaphoreType.DMA],
        name="pick",
    )(slot, shares, right_stats)

    picked = picked.reshape(near * groups, halves, TILE_ROWS, LANES)
    own = lax.all_to_all(picked, ("zl", "y", "x"), 0, 0, tiled=True)
    own = own.reshape(near, groups, halves, TILE_ROWS, LANES)
    other = lax.ppermute(own, "core", [(0, 1), (1, 0)])

    operands = tuple(
        pltpu.with_memory_space_constraint(a, pltpu.VMEM)
        for a in (left_stats, right_stats, left_root, right_root)
    )
    results = owner_call(True, (own, *operands), slots, band, order)
    return owner_call(False, (other, *operands, *results), slots, band, order)


def solution(mesh):
    fine = Mesh(mesh.devices.reshape(8, 4, 4, 4, 2), ("cube", "zl", "y", "x", "core"))
    shard, replica = ("cube", "zl", "y"), ("x", "core")
    in_specs = (
        P(replica, shard, None),
        P(),
        P(),
        P(),
        P(shard, replica, None),
        P(shard, replica, None),
        P(shard, None, None),
        P(shard, None, None),
    )
    out_specs = (P(shard, replica, None),) * 3
    return jax.shard_map(
        per_device, mesh=fine, in_specs=in_specs, out_specs=out_specs, check_vma=False
    )
```

```python
import functools

import jax
import jax.numpy as jnp
from jax import lax
from jax.experimental import pallas as pl
from jax.experimental.pallas import tpu as pltpu
from jax.sharding import Mesh, PartitionSpec as P

TILE_ROWS = 16
LANES = 128


def vmem(n):
    return [pl.BlockSpec(memory_space=pltpu.VMEM)] * n


def cut_kernel(
    owner_hbm, row_hbm, col_hbm, grads_hbm, parts_ref, slot_ref,
    owner_ref, row_ref, col_ref, grads_ref, count_ref, table_sem, grads_sem, *, near, slots, ncb,
):
    grads_copy = pltpu.make_async_copy(grads_hbm, grads_ref, grads_sem)
    grads_copy.start()
    table_copies = [
        pltpu.make_async_copy(source, target, table_sem.at[i])
        for i, (source, target) in enumerate(((owner_hbm, owner_ref), (row_hbm, row_ref), (col_hbm, col_ref)))
    ]
    for copy in table_copies:
        copy.start()
    halves = grads_ref.shape[1] // TILE_ROWS
    for i in range(slot_ref.shape[0]):
        slot_ref[i] = -1
    for i in range(count_ref.shape[0]):
        count_ref[i] = 0
    base = lax.axis_index("cube") * near
    for copy in table_copies:
        copy.wait()

    def put(b, carry):
        local = owner_ref[b] - base
        mine = (local >= 0) & (local < near)
        local = jnp.where(mine, local, near)
        rank = count_ref[local]
        slot_ref[local * slots + rank] = row_ref[b] * (halves * ncb) + col_ref[b]
        count_ref[local] = rank + mine.astype(jnp.int32)
        return carry

    lax.fori_loop(0, owner_ref.shape[0], put, 0, unroll=8)
    grads_copy.wait()
    order = grads_ref.shape[2] // ncb
    groups = order // LANES
    for group in range(groups):
        for half in range(halves):
            for b in range(ncb):
                parts_ref[group * halves + half, b] = grads_ref[
                    0, pl.ds(half * TILE_ROWS, TILE_ROWS), pl.ds(b * order + group * LANES, LANES)
                ]


def pick_kernel(slot_ref, shares_ref, picked_ref, *, ncb):
    near, groups, halves = picked_ref.shape[:3]
    core = lax.axis_index("core")
    for o in range(near):
        at = slot_ref[o * 2 + core]
        for half in range(halves):
            tile = shares_ref[jnp.maximum(at, 0) + half * ncb]
            tile = jnp.where(at >= 0, tile, jnp.zeros_like(tile))
            for x in range(groups):
                picked_ref[o, x, half] = tile


def owner_kernel(
    tiles_ref, left_stats_ref, right_stats_ref, right_root_ref, left_root_ref, *refs, mine
):
    if mine:
        direction_hbm, left_hbm, right_hbm, staged_ref, roots_ref, roots_sem = refs[:6]
    else:
        direction_hbm, left_hbm, right_hbm = refs[3:6]
        roots_ref = left_root_ref
    block_ref, columns_ref, direction_ref, left_ref, right_ref, out_sem = refs[-6:]
    near, groups, halves = tiles_ref.shape[:3]
    order = block_ref.shape[0]
    band = left_ref.shape[0]
    core = lax.axis_index("core")
    me = lax.axis_index("x") * 2 + core
    k = core if mine else 1 - core
    my_rows = pl.ds(pl.multiple_of(me * band, band), band)
    copies = []
    if mine:
        copies = [
            pltpu.make_async_copy(left_root_ref.at[k, my_rows, :], roots_ref, roots_sem.at[0]),
            pltpu.make_async_copy(left_root_ref.at[1 - k, my_rows, :], staged_ref, roots_sem.at[1]),
        ]
        for copy in copies:
            copy.start()
    for j in range(near):
        for c in range(groups):
            for half in range(halves):
                rows = pl.ds((j * halves + half) * TILE_ROWS, TILE_ROWS)
                block_ref[rows, pl.ds(c * LANES, LANES)] = tiles_ref[j, c, half]
    block = block_ref[...]
    results = [
        pltpu.make_async_copy(src, dst.at[k], out_sem.at[i])
        for i, (src, dst) in enumerate(
            ((left_ref, left_hbm), (right_ref, right_hbm), (direction_ref, direction_hbm))
        )
    ]
    rows = block_ref[my_rows, :]
    left = lax.dot_general(rows, block, (((1,), (1,)), ((), ())), preferred_element_type=jnp.float32)
    left_ref[...] = 0.8 * left_stats_ref[k] + (0.2 / order) * left
    results[0].start()
    start = pl.multiple_of((me * band // LANES) * LANES, LANES)
    two_bands = block_ref[:, pl.ds(start, LANES)]
    columns_ref[...] = lax.dot_general(
        two_bands, block, (((0,), (0,)), ((), ())), preferred_element_type=jnp.float32
    )
    right = columns_ref[pl.ds(pl.multiple_of(me * band - start, band), band), :]
    right_ref[...] = 0.8 * right_stats_ref[k] + (0.2 / order) * right
    results[1].start()
    mixed = jnp.dot(block, right_root_ref[k], preferred_element_type=jnp.float32).astype(jnp.bfloat16)
    for copy in copies:
        copy.wait()
    direction_ref[...] = jnp.dot(
        roots_ref[...], mixed, preferred_element_type=jnp.float32
    ).astype(jnp.bfloat16)
    results[2].start()
    for copy in results:
        copy.wait()


def owner_call(mine, operands, slots, band, order):
    bf16, f32 = jnp.bfloat16, jnp.float32
    hbm = pl.BlockSpec(memory_space=pl.ANY)
    out_shape = tuple(jax.ShapeDtypeStruct((slots, band, order), t) for t in (bf16, f32, f32))
    out_specs = (hbm,) * 3
    scratch = []
    if mine:
        in_specs = vmem(4) + [hbm]
        out_shape += (pltpu.VMEM((band, order), bf16),)
        out_specs += tuple(vmem(1))
        scratch = [pltpu.VMEM((band, order), bf16), pltpu.SemaphoreType.DMA((2,))]
        aliases = {}
    else:
        in_specs = vmem(5) + [hbm] * 3
        aliases = {5: 0, 6: 1, 7: 2}
    scratch += [
        pltpu.VMEM((order, order), bf16),
        pltpu.VMEM((LANES, order), f32),
        pltpu.VMEM((band, order), bf16),
        pltpu.VMEM((band, order), f32),
        pltpu.VMEM((band, order), f32),
        pltpu.SemaphoreType.DMA((3,)),
    ]
    return pl.pallas_call(
        functools.partial(owner_kernel, mine=mine),
        out_shape=out_shape,
        in_specs=in_specs,
        out_specs=out_specs,
        scratch_shapes=scratch,
        input_output_aliases=aliases,
        compiler_params=pltpu.CompilerParams(vmem_limit_bytes=32 * 1024 * 1024),
        cost_estimate=pl.CostEstimate(
            flops=2 * order * order * (order + 4 * band), bytes_accessed=8 * order * order, transcendentals=0
        ),
        name="own" if mine else "other",
    )(*operands)


def per_device(
    replica_grads, block_row, block_col, block_owner, left_stats, right_stats, left_root, right_root
):
    slots, order, _ = left_root.shape
    band = left_stats.shape[1]
    ncb = replica_grads.shape[2] // order
    groups, halves = lax.axis_size("x"), lax.axis_size("core")
    replicas = groups * halves
    near = lax.axis_size("zl") * lax.axis_size("y")
    bf16 = jnp.bfloat16
    smem = pl.BlockSpec(memory_space=pltpu.SMEM)

    parts, slot = pl.pallas_call(
        functools.partial(cut_kernel, near=near, slots=slots, ncb=ncb),
        out_shape=(
            pltpu.VMEM((replicas, ncb, TILE_ROWS, LANES), bf16),
            jax.ShapeDtypeStruct(((near + 1) * slots,), jnp.int32),
        ),
        in_specs=[pl.BlockSpec(memory_space=pl.ANY)] * 4,
        out_specs=(vmem(1)[0], smem),
        scratch_shapes=[pltpu.SMEM(block_owner.shape, jnp.int32)] * 3
        + [
            pltpu.VMEM(replica_grads.shape, bf16),
            pltpu.SMEM((near + 1,), jnp.int32),
            pltpu.SemaphoreType.DMA((3,)),
            pltpu.SemaphoreType.DMA,
        ],
        name="cut",
    )(block_owner, block_row, block_col, replica_grads)

    received = lax.all_to_all(parts, ("x", "core"), 0, 0, tiled=True)
    summed = jnp.sum(received.astype(jnp.float32), axis=0).astype(bf16)
    shares = lax.all_gather(summed, ("cube", "core"), axis=0, tiled=True)
    shares = pltpu.with_memory_space_constraint(shares, pltpu.VMEM)

    picked = pl.pallas_call(
        functools.partial(pick_kernel, ncb=ncb),
        out_shape=pltpu.VMEM((near, groups, halves, TILE_ROWS, LANES), bf16),
        in_specs=[smem] + vmem(1),
        out_specs=vmem(1)[0],
        name="pick",
    )(slot, shares)

    picked = picked.reshape(near * groups, halves, TILE_ROWS, LANES)
    own = lax.all_to_all(picked, ("zl", "y", "x"), 0, 0, tiled=True)
    own = own.reshape(near, groups, halves, TILE_ROWS, LANES)
    other = lax.ppermute(own, "core", [(0, 1), (1, 0)])

    operands = tuple(
        pltpu.with_memory_space_constraint(a, pltpu.VMEM) for a in (left_stats, right_stats, right_root)
    )
    left_root = pltpu.with_memory_space_constraint(left_root, pltpu.HBM)
    *results, staged = owner_call(True, (own, *operands, left_root), slots, band, order)
    return owner_call(False, (other, *operands, staged, *results), slots, band, order)


def solution(mesh):
    fine = Mesh(mesh.devices.reshape(8, 4, 4, 4, 2), ("cube", "zl", "y", "x", "core"))
    shard, replica = ("cube", "zl", "y"), ("x", "core")
    in_specs = (
        P(replica, shard, None),
        P(),
        P(),
        P(),
        P(shard, replica, None),
        P(shard, replica, None),
        P(shard, None, None),
        P(shard, None, None),
    )
    out_specs = (P(shard, replica, None),) * 3
    return jax.shard_map(
        per_device, mesh=fine, in_specs=in_specs, out_specs=out_specs, check_vma=False
    )
```

```python
import functools

import jax
import jax.numpy as jnp
from jax import lax
from jax.experimental import pallas as pl
from jax.experimental.pallas import tpu as pltpu
from jax.sharding import Mesh, PartitionSpec as P

TILE_ROWS = 16
LANES = 128


def vmem(n):
    return [pl.BlockSpec(memory_space=pltpu.VMEM)] * n


def cut_kernel(
    owner_hbm, row_hbm, col_hbm, grads_hbm, parts_ref, slot_ref,
    owner_ref, row_ref, col_ref, grads_ref, count_ref, table_sem, grads_sem, *, near, slots, ncb,
):
    table_copies = [
        pltpu.make_async_copy(source, target, table_sem.at[i])
        for i, (source, target) in enumerate(((owner_hbm, owner_ref), (row_hbm, row_ref), (col_hbm, col_ref)))
    ]
    for copy in table_copies:
        copy.start()
    grads_copy = pltpu.make_async_copy(grads_hbm, grads_ref, grads_sem)
    grads_copy.start()
    halves = grads_ref.shape[1] // TILE_ROWS
    for i in range(slot_ref.shape[0]):
        slot_ref[i] = -1
    for i in range(count_ref.shape[0]):
        count_ref[i] = 0
    base = lax.axis_index("cube") * near
    for copy in table_copies:
        copy.wait()

    def put(b, carry):
        local = owner_ref[b] - base
        mine = (local >= 0) & (local < near)
        local = jnp.where(mine, local, near)
        rank = count_ref[local]
        slot_ref[local * slots + rank] = row_ref[b] * (halves * ncb) + col_ref[b]
        count_ref[local] = rank + mine.astype(jnp.int32)
        return carry

    lax.fori_loop(0, owner_ref.shape[0], put, 0, unroll=8)
    grads_copy.wait()
    order = grads_ref.shape[2] // ncb
    groups = order // LANES
    for group in range(groups):
        for half in range(halves):
            for b in range(ncb):
                parts_ref[group * halves + half, b] = grads_ref[
                    0, pl.ds(half * TILE_ROWS, TILE_ROWS), pl.ds(b * order + group * LANES, LANES)
                ]


def pick_kernel(slot_ref, shares_ref, picked_ref, *, ncb):
    near, groups, halves = picked_ref.shape[:3]
    core = lax.axis_index("core")
    for o in range(near):
        at = slot_ref[o * 2 + core]
        for half in range(halves):
            tile = shares_ref[jnp.maximum(at, 0) + half * ncb]
            tile = jnp.where(at >= 0, tile, jnp.zeros_like(tile))
            for x in range(groups):
                picked_ref[o, x, half] = tile


def owner_kernel(
    tiles_ref, left_stats_ref, right_stats_ref, right_root_ref, left_root_ref, *refs, mine
):
    if mine:
        direction_hbm, left_hbm, right_hbm, staged_ref, roots_ref, roots_sem = refs[:6]
    else:
        direction_hbm, left_hbm, right_hbm = refs[3:6]
        roots_ref = left_root_ref
    block_ref, columns_ref, direction_ref, left_ref, right_ref, out_sem = refs[-6:]
    near, groups, halves = tiles_ref.shape[:3]
    order = block_ref.shape[0]
    band = left_ref.shape[0]
    core = lax.axis_index("core")
    me = lax.axis_index("x") * 2 + core
    k = core if mine else 1 - core
    my_rows = pl.ds(pl.multiple_of(me * band, band), band)
    copies = []
    if mine:
        copies = [
            pltpu.make_async_copy(left_root_ref.at[k, my_rows, :], roots_ref, roots_sem.at[0]),
            pltpu.make_async_copy(left_root_ref.at[1 - k, my_rows, :], staged_ref, roots_sem.at[1]),
        ]
        for copy in copies:
            copy.start()
    for j in range(near):
        for c in range(groups):
            for half in range(halves):
                rows = pl.ds((j * halves + half) * TILE_ROWS, TILE_ROWS)
                block_ref[rows, pl.ds(c * LANES, LANES)] = tiles_ref[j, c, half]
    block = block_ref[...]
    results = [
        pltpu.make_async_copy(src, dst.at[k], out_sem.at[i])
        for i, (src, dst) in enumerate(
            ((left_ref, left_hbm), (right_ref, right_hbm), (direction_ref, direction_hbm))
        )
    ]
    rows = block_ref[my_rows, :]
    left = lax.dot_general(rows, block, (((1,), (1,)), ((), ())), preferred_element_type=jnp.float32)
    left_ref[...] = 0.8 * left_stats_ref[k] + (0.2 / order) * left
    results[0].start()
    start = pl.multiple_of((me * band // LANES) * LANES, LANES)
    two_bands = block_ref[:, pl.ds(start, LANES)]
    columns_ref[...] = lax.dot_general(
        two_bands, block, (((0,), (0,)), ((), ())), preferred_element_type=jnp.float32
    )
    right = columns_ref[pl.ds(pl.multiple_of(me * band - start, band), band), :]
    right_ref[...] = 0.8 * right_stats_ref[k] + (0.2 / order) * right
    results[1].start()
    for copy in copies[:1]:
        copy.wait()
    mixed = jnp.dot(roots_ref[...], block, preferred_element_type=jnp.float32).astype(jnp.bfloat16)
    direction_ref[...] = jnp.dot(
        mixed, right_root_ref[k], preferred_element_type=jnp.float32
    ).astype(jnp.bfloat16)
    results[2].start()
    for copy in copies[1:] + results:
        copy.wait()


def owner_call(mine, operands, slots, band, order):
    bf16, f32 = jnp.bfloat16, jnp.float32
    hbm = pl.BlockSpec(memory_space=pl.ANY)
    out_shape = tuple(jax.ShapeDtypeStruct((slots, band, order), t) for t in (bf16, f32, f32))
    out_specs = (hbm,) * 3
    scratch = []
    if mine:
        in_specs = vmem(4) + [hbm]
        out_shape += (pltpu.VMEM((band, order), bf16),)
        out_specs += tuple(vmem(1))
        scratch = [pltpu.VMEM((band, order), bf16), pltpu.SemaphoreType.DMA((2,))]
        aliases = {}
    else:
        in_specs = vmem(5) + [hbm] * 3
        aliases = {5: 0, 6: 1, 7: 2}
    scratch += [
        pltpu.VMEM((order, order), bf16),
        pltpu.VMEM((LANES, order), f32),
        pltpu.VMEM((band, order), bf16),
        pltpu.VMEM((band, order), f32),
        pltpu.VMEM((band, order), f32),
        pltpu.SemaphoreType.DMA((3,)),
    ]
    return pl.pallas_call(
        functools.partial(owner_kernel, mine=mine),
        out_shape=out_shape,
        in_specs=in_specs,
        out_specs=out_specs,
        scratch_shapes=scratch,
        input_output_aliases=aliases,
        compiler_params=pltpu.CompilerParams(vmem_limit_bytes=32 * 1024 * 1024),
        cost_estimate=pl.CostEstimate(
            flops=2 * order * order * 5 * band, bytes_accessed=8 * order * order, transcendentals=0
        ),
        name="own" if mine else "other",
    )(*operands)


def per_device(
    replica_grads, block_row, block_col, block_owner, left_stats, right_stats, left_root, right_root
):
    slots, order, _ = left_root.shape
    band = left_stats.shape[1]
    ncb = replica_grads.shape[2] // order
    groups, halves = lax.axis_size("x"), lax.axis_size("core")
    replicas = groups * halves
    near = lax.axis_size("zl") * lax.axis_size("y")
    bf16 = jnp.bfloat16
    smem = pl.BlockSpec(memory_space=pltpu.SMEM)

    parts, slot = pl.pallas_call(
        functools.partial(cut_kernel, near=near, slots=slots, ncb=ncb),
        out_shape=(
            pltpu.VMEM((replicas, ncb, TILE_ROWS, LANES), bf16),
            jax.ShapeDtypeStruct(((near + 1) * slots,), jnp.int32),
        ),
        in_specs=[pl.BlockSpec(memory_space=pl.ANY)] * 4,
        out_specs=(vmem(1)[0], smem),
        scratch_shapes=[pltpu.SMEM(block_owner.shape, jnp.int32)] * 3
        + [
            pltpu.VMEM(replica_grads.shape, bf16),
            pltpu.SMEM((near + 1,), jnp.int32),
            pltpu.SemaphoreType.DMA((3,)),
            pltpu.SemaphoreType.DMA,
        ],
        name="cut",
    )(block_owner, block_row, block_col, replica_grads)

    received = lax.all_to_all(parts, ("x", "core"), 0, 0, tiled=True)
    summed = jnp.sum(received.astype(jnp.float32), axis=0).astype(bf16)
    shares = lax.all_gather(summed, ("cube", "core"), axis=0, tiled=True)
    shares = pltpu.with_memory_space_constraint(shares, pltpu.VMEM)

    picked = pl.pallas_call(
        functools.partial(pick_kernel, ncb=ncb),
        out_shape=pltpu.VMEM((near, groups, halves, TILE_ROWS, LANES), bf16),
        in_specs=[smem] + vmem(1),
        out_specs=vmem(1)[0],
        name="pick",
    )(slot, shares)

    picked = picked.reshape(near * groups, halves, TILE_ROWS, LANES)
    own = lax.all_to_all(picked, ("zl", "y", "x"), 0, 0, tiled=True)
    own = own.reshape(near, groups, halves, TILE_ROWS, LANES)
    other = lax.ppermute(own, "core", [(0, 1), (1, 0)])

    operands = tuple(
        pltpu.with_memory_space_constraint(a, pltpu.VMEM) for a in (left_stats, right_stats, right_root)
    )
    left_root = pltpu.with_memory_space_constraint(left_root, pltpu.HBM)
    *results, staged = owner_call(True, (own, *operands, left_root), slots, band, order)
    return owner_call(False, (other, *operands, staged, *results), slots, band, order)


def solution(mesh):
    fine = Mesh(mesh.devices.reshape(8, 4, 4, 4, 2), ("cube", "zl", "y", "x", "core"))
    shard, replica = ("cube", "zl", "y"), ("x", "core")
    in_specs = (
        P(replica, shard, None),
        P(),
        P(),
        P(),
        P(shard, replica, None),
        P(shard, replica, None),
        P(shard, None, None),
        P(shard, None, None),
    )
    out_specs = (P(shard, replica, None),) * 3
    return jax.shard_map(
        per_device, mesh=fine, in_specs=in_specs, out_specs=out_specs, check_vma=False
    )
```

```python
import functools

import jax
import jax.numpy as jnp
from jax import lax
from jax.experimental import pallas as pl
from jax.experimental.pallas import tpu as pltpu
from jax.sharding import Mesh, PartitionSpec as P

TILE_ROWS = 16
LANES = 128


def vmem(n):
    return [pl.BlockSpec(memory_space=pltpu.VMEM)] * n


def cut_kernel(
    owner_hbm, row_hbm, col_hbm, grads_hbm, parts_ref, slot_ref,
    owner_ref, row_ref, col_ref, grads_ref, count_ref, table_sem, grads_sem, *, near, slots, ncb,
):
    table_copies = [
        pltpu.make_async_copy(source, target, table_sem.at[i])
        for i, (source, target) in enumerate(((owner_hbm, owner_ref), (row_hbm, row_ref), (col_hbm, col_ref)))
    ]
    for copy in table_copies:
        copy.start()
    grads_copy = pltpu.make_async_copy(grads_hbm, grads_ref, grads_sem)
    grads_copy.start()
    halves = grads_ref.shape[1] // TILE_ROWS
    for i in range(slot_ref.shape[0]):
        slot_ref[i] = -1
    for i in range(count_ref.shape[0]):
        count_ref[i] = 0
    base = lax.axis_index("cube") * near
    for copy in table_copies:
        copy.wait()

    def put(b, carry):
        local = owner_ref[b] - base
        mine = (local >= 0) & (local < near)
        local = jnp.where(mine, local, near)
        rank = count_ref[local]
        slot_ref[local * slots + rank] = row_ref[b] * (halves * ncb) + col_ref[b]
        count_ref[local] = rank + mine.astype(jnp.int32)
        return carry

    lax.fori_loop(0, owner_ref.shape[0], put, 0, unroll=8)
    grads_copy.wait()
    order = grads_ref.shape[2] // ncb
    groups = order // LANES
    for group in range(groups):
        for half in range(halves):
            for b in range(ncb):
                parts_ref[group * halves + half, b] = grads_ref[
                    0, pl.ds(half * TILE_ROWS, TILE_ROWS), pl.ds(b * order + group * LANES, LANES)
                ]


def pick_kernel(slot_ref, shares_ref, _, picked_ref, *, ncb):
    near, groups, halves = picked_ref.shape[:3]
    core = lax.axis_index("core")
    for o in range(near):
        at = slot_ref[o * 2 + core]
        for half in range(halves):
            tile = shares_ref[jnp.maximum(at, 0) + half * ncb]
            tile = jnp.where(at >= 0, tile, jnp.zeros_like(tile))
            for x in range(groups):
                picked_ref[o, x, half] = tile


def owner_kernel(
    tiles_ref, left_stats_ref, right_stats_ref, left_root_ref, right_root_ref, *refs, mine
):
    direction_hbm, left_hbm, right_hbm = refs[-9:-6]
    block_ref, columns_ref, direction_ref, left_ref, right_ref, out_sem = refs[-6:]
    near, groups, halves = tiles_ref.shape[:3]
    order = block_ref.shape[0]
    band = left_ref.shape[0]
    core = lax.axis_index("core")
    me = lax.axis_index("x") * 2 + core
    k = core if mine else 1 - core
    my_rows = pl.ds(pl.multiple_of(me * band, band), band)
    for j in range(near):
        for c in range(groups):
            for half in range(halves):
                rows = pl.ds((j * halves + half) * TILE_ROWS, TILE_ROWS)
                block_ref[rows, pl.ds(c * LANES, LANES)] = tiles_ref[j, c, half]
    block = block_ref[...]
    results = [
        pltpu.make_async_copy(src, dst.at[k], out_sem.at[i])
        for i, (src, dst) in enumerate(
            ((left_ref, left_hbm), (right_ref, right_hbm), (direction_ref, direction_hbm))
        )
    ]
    rows = block_ref[my_rows, :]
    left = lax.dot_general(rows, block, (((1,), (1,)), ((), ())), preferred_element_type=jnp.float32)
    left_ref[...] = 0.8 * left_stats_ref[k] + (0.2 / order) * left
    results[0].start()
    start = pl.multiple_of((me * band // LANES) * LANES, LANES)
    two_bands = block_ref[:, pl.ds(start, LANES)]
    columns_ref[...] = lax.dot_general(
        two_bands, block, (((0,), (0,)), ((), ())), preferred_element_type=jnp.float32
    )
    right = columns_ref[pl.ds(pl.multiple_of(me * band - start, band), band), :]
    right_ref[...] = 0.8 * right_stats_ref[k] + (0.2 / order) * right
    results[1].start()
    mixed = jnp.dot(left_root_ref[k, my_rows, :], block, preferred_element_type=jnp.float32).astype(jnp.bfloat16)
    direction_ref[...] = jnp.dot(
        mixed, right_root_ref[k], preferred_element_type=jnp.float32
    ).astype(jnp.bfloat16)
    results[2].start()
    for copy in results:
        copy.wait()


def owner_call(mine, operands, slots, band, order):
    bf16, f32 = jnp.bfloat16, jnp.float32
    hbm = pl.BlockSpec(memory_space=pl.ANY)
    aliases = {} if mine else {5: 0, 6: 1, 7: 2}
    scratch = [
        pltpu.VMEM((order, order), bf16),
        pltpu.VMEM((LANES, order), f32),
        pltpu.VMEM((band, order), bf16),
        pltpu.VMEM((band, order), f32),
        pltpu.VMEM((band, order), f32),
        pltpu.SemaphoreType.DMA((3,)),
    ]
    return pl.pallas_call(
        functools.partial(owner_kernel, mine=mine),
        out_shape=tuple(jax.ShapeDtypeStruct((slots, band, order), t) for t in (bf16, f32, f32)),
        in_specs=vmem(5) + [hbm] * len(aliases),
        out_specs=(hbm,) * 3,
        scratch_shapes=scratch,
        input_output_aliases=aliases,
        compiler_params=pltpu.CompilerParams(vmem_limit_bytes=32 * 1024 * 1024),
        cost_estimate=pl.CostEstimate(
            flops=2 * order * order * 5 * band, bytes_accessed=8 * order * order, transcendentals=0
        ),
        name="own" if mine else "other",
    )(*operands)


def per_device(
    replica_grads, block_row, block_col, block_owner, left_stats, right_stats, left_root, right_root
):
    slots, order, _ = left_root.shape
    band = left_stats.shape[1]
    ncb = replica_grads.shape[2] // order
    groups, halves = lax.axis_size("x"), lax.axis_size("core")
    replicas = groups * halves
    near = lax.axis_size("zl") * lax.axis_size("y")
    bf16 = jnp.bfloat16
    smem = pl.BlockSpec(memory_space=pltpu.SMEM)

    parts, slot = pl.pallas_call(
        functools.partial(cut_kernel, near=near, slots=slots, ncb=ncb),
        out_shape=(
            pltpu.VMEM((replicas, ncb, TILE_ROWS, LANES), bf16),
            jax.ShapeDtypeStruct(((near + 1) * slots,), jnp.int32),
        ),
        in_specs=[pl.BlockSpec(memory_space=pl.ANY)] * 4,
        out_specs=(vmem(1)[0], smem),
        scratch_shapes=[pltpu.SMEM(block_owner.shape, jnp.int32)] * 3
        + [
            pltpu.VMEM(replica_grads.shape, bf16),
            pltpu.SMEM((near + 1,), jnp.int32),
            pltpu.SemaphoreType.DMA((3,)),
            pltpu.SemaphoreType.DMA,
        ],
        name="cut",
    )(block_owner, block_row, block_col, replica_grads)

    received = lax.all_to_all(parts, ("x", "core"), 0, 0, tiled=True)
    summed = jnp.sum(received.astype(jnp.float32), axis=0).astype(bf16)
    shares = lax.all_gather(summed, ("cube", "core"), axis=0, tiled=True)
    shares = pltpu.with_memory_space_constraint(shares, pltpu.VMEM)

    left_stats, right_stats, left_root, right_root = (
        pltpu.with_memory_space_constraint(a, pltpu.VMEM)
        for a in (left_stats, right_stats, left_root, right_root)
    )
    picked = pl.pallas_call(
        functools.partial(pick_kernel, ncb=ncb),
        out_shape=pltpu.VMEM((near, groups, halves, TILE_ROWS, LANES), bf16),
        in_specs=[smem] + vmem(2),
        out_specs=vmem(1)[0],
        name="pick",
    )(slot, shares, right_root)

    picked = picked.reshape(near * groups, halves, TILE_ROWS, LANES)
    own = lax.all_to_all(picked, ("zl", "y", "x"), 0, 0, tiled=True)
    own = own.reshape(near, groups, halves, TILE_ROWS, LANES)
    other = lax.ppermute(own, "core", [(0, 1), (1, 0)])

    operands = left_stats, right_stats, left_root, right_root
    results = owner_call(True, (own, *operands), slots, band, order)
    return owner_call(False, (other, *operands, *results), slots, band, order)


def solution(mesh):
    fine = Mesh(mesh.devices.reshape(8, 4, 4, 4, 2), ("cube", "zl", "y", "x", "core"))
    shard, replica = ("cube", "zl", "y"), ("x", "core")
    in_specs = (
        P(replica, shard, None),
        P(),
        P(),
        P(),
        P(shard, replica, None),
        P(shard, replica, None),
        P(shard, None, None),
        P(shard, None, None),
    )
    out_specs = (P(shard, replica, None),) * 3
    return jax.shard_map(
        per_device, mesh=fine, in_specs=in_specs, out_specs=out_specs, check_vma=False
    )
```
